256 devices in a mesh: pts: 32 (over z_hi, x, core), modes: 8 (over y, z_lo).
Axes of the slice: x: 4, y: 4, z: 8 (z_hi: 4, z_lo: 2; z = z_hi * 2 + z_lo), core: 2. Of those that a mesh axis runs over, the one named last changes fastest.
Arguments:
- features: bfloat16 [131072, 128], P('pts'), may hold values from -6 to 6
- coords: float32 [3, 131072], P(None, 'pts'), may hold values from 0 to 1
- quad_weight: float32 [131072], P('pts'), may hold values from 0.5 to 6, as said below
- mode_table: int32 [3, 8192], replicated, may hold values from -8 to 31, as said below
- mode_weight: bfloat16 [8192, 2, 128, 128], P(('pts', 'modes')), may hold values from -5 to 5
- lin_weight: bfloat16 [128, 128], replicated, may hold values from -0.5 to 0.5
- bias: float32 [128], replicated, may hold values from -3 to 3
Outputs:
- output: bfloat16 [131072, 128], P(('pts', 'modes'))
The draws below stay inside these ranges and needn't reach their ends.
Inputs may be any that keep to these rules, and one draw needn't show every extreme that they name: `mode_table`: each column is a distinct triple (kx, ky, kz) with -8 <= kx < 8, -8 <= ky < 8, 0 <= kz < 32; every such triple appears exactly once, in an order drawn from the seed. `quad_weight`: Positive.
All inputs are finite; a program needn't handle non-finite values.
Results may differ from the reference program's by a relative error of at most 0.018.
Values may be sent and summed in bfloat16 or wider, within the bound.
No kernel may reach another device: no remote copies, remote signals or barrier semaphores. Data moves between devices by JAX's collectives and lax.ppermute only.
A program may use at most 64 MiB of HBM per device.

```python
import math
import jax
import jax.numpy as jnp
from jax import lax

C = 128
MX = 16
MY = 16
MZ = 32
MODES = 8192
TOTAL = 131072


def draw_quad_weight(key, part):
    ramp = 1.0 + 2.0 * jnp.arange(TOTAL, dtype=jnp.float32) / (TOTAL - 1)
    base = jnp.exp(jax.random.uniform(key, (TOTAL,), jnp.float32, jnp.log(0.5), jnp.log(2.0)))
    return jnp.clip(base * ramp, 0.5, 6.0).astype(jnp.float32)


def draw_mode_table(key, part):
    order = jax.random.permutation(jax.random.fold_in(key, 7), MODES).astype(jnp.int32)
    kx_num = order // (MY * MZ) - MX // 2
    ky_num = order // MZ % MY - MY // 2
    kz_num = order % MZ
    return jnp.stack([kx_num, ky_num, kz_num]).astype(jnp.int32)


def block_scale(stream_key, extent, pieces, low, top_value):
    level, own = 1.0, jax.random.fold_in(stream_key, 6)
    for dim, blocks in pieces:
        draws = jnp.exp(jax.random.uniform(jax.random.fold_in(own, dim), (blocks,), jnp.float32, low / len(pieces), top_value / len(pieces)))
        level = level * jnp.repeat(draws, extent[dim] // blocks).reshape([-1 if axis == dim else 1 for axis in range(len(extent))])
    return level


def gaussian(rng, extent, scale, limit, shards=(), kind=jnp.bfloat16):
    values = scale * jax.random.normal(rng, extent, jnp.float32)
    if shards:
        values = values * block_scale(rng, extent, shards, -0.22, 0.18)
    return jnp.clip(values, -limit, limit).astype(kind)


def setup_inputs(seed: int = 0) -> dict:
    streams_of = jax.random.split(jax.random.key(seed), 8)
    features = gaussian(streams_of[0], (TOTAL, C), 1.0, 6.0, ((0, 32),))
    coords = jnp.clip(1.0 * jax.random.uniform(streams_of[1], (3, TOTAL), jnp.float32) ** block_scale(streams_of[1], (3, TOTAL), ((1, 32),), -0.2, 0.2), 0.0, 1.0)
    quad_weight = draw_quad_weight(jax.random.fold_in(streams_of[7], 71), 0)
    mode_table = draw_mode_table(jax.random.fold_in(streams_of[7], 71), 0)
    mode_weight = gaussian(streams_of[4], (MODES, 2, C, C), ((TOTAL / (MODES * C)) ** 0.5), 5.0, ((0, 256),))
    lin_weight = gaussian(streams_of[5], (C, C), C ** -0.5, 0.5)
    bias = gaussian(streams_of[6], (C,), 0.5, 3.0, (), jnp.float32)
    return {"features": features, "coords": coords, "quad_weight": quad_weight, "mode_table": mode_table, "mode_weight": mode_weight, "lin_weight": lin_weight, "bias": bias}


def phase_basis(coords, wave):
    turns = coords[0][:, None] * wave[0][None, :] + coords[1][:, None] * wave[1][None, :]
    turns = turns + coords[2][:, None] * wave[2][None, :]
    angle = (2.0 * math.pi) * turns
    return jnp.concatenate([jnp.cos(angle), -jnp.sin(angle)], axis=1).astype(jnp.bfloat16)


def reference(features, coords, quad_weight, mode_table, mode_weight, lin_weight, bias):
    weighted = (quad_weight[:, None] * features.astype(jnp.float32)).astype(jnp.bfloat16)
    total = jnp.sum(quad_weight)
    wave = mode_table.astype(jnp.float32)
    blocks = MODES // 256
    wave_blocks = wave.reshape(3, blocks, 256).transpose(1, 0, 2)
    weighted_f = weighted.astype(jnp.float32)

    def analyse(part_wave):
        basis = phase_basis(coords, part_wave).astype(jnp.float32)
        res = lax.dot_general(basis, weighted_f, (((0,), (0,)), ((), ())), preferred_element_type=jnp.float32)
        return res.reshape(2, 256, C).transpose(1, 0, 2).reshape(256, 2 * C)

    coef = lax.map(analyse, wave_blocks).reshape(MODES, 2 * C).astype(jnp.bfloat16)
    real_in = coef[:, :C].astype(jnp.float32)
    imag_in = coef[:, C:].astype(jnp.float32)
    w_real = mode_weight[:, 0].astype(jnp.float32)
    w_imag = mode_weight[:, 1].astype(jnp.float32)
    real_out = jnp.einsum("mc,mcd->md", real_in, w_real) - jnp.einsum("mc,mcd->md", imag_in, w_imag)
    imag_out = jnp.einsum("mc,mcd->md", real_in, w_imag) + jnp.einsum("mc,mcd->md", imag_in, w_real)
    filtered = jnp.concatenate([real_out, imag_out], axis=1).astype(jnp.bfloat16)
    filt_blocks = filtered.reshape(blocks, 256, 2 * C)

    def synthesize(carry, inputs):
        part_wave, piece = inputs
        basis = phase_basis(coords, part_wave).astype(jnp.float32)
        rhs = jnp.concatenate([piece[:, :C], piece[:, C:]], axis=0).astype(jnp.float32)
        return carry + jnp.dot(basis, rhs, preferred_element_type=jnp.float32), None

    spectral, unused = lax.scan(synthesize, jnp.zeros((TOTAL, C), jnp.float32), (wave_blocks, filt_blocks))
    linear = jnp.dot(features, lin_weight, preferred_element_type=jnp.float32)
    pre = spectral / total + linear + bias[None, :]
    return jax.nn.gelu(pre, approximate=False).astype(jnp.bfloat16)
```

```python
import math

import jax
import jax.numpy as jnp
from jax import lax
from jax.sharding import Mesh, PartitionSpec as P

SIZES = {"z_hi": 4, "x": 4, "core": 2, "y": 4, "z_lo": 2}
PTS = ("z_hi", "x", "core")
GRP = ("y", "z_lo")
ALL = PTS + GRP


def phase_basis(coords, wave):
    turns = coords[0][:, None] * wave[0][None, :] + coords[1][:, None] * wave[1][None, :]
    turns = turns + coords[2][:, None] * wave[2][None, :]
    angle = 2.0 * math.pi * turns
    return jnp.concatenate([jnp.cos(angle), -jnp.sin(angle)], axis=1).astype(jnp.bfloat16)


def send(value, axes, shift):
    n = 1
    for a in axes:
        n *= SIZES[a]
    return lax.ppermute(value, axes, [(j, (j + shift) % n) for j in range(n)])


def split3(value):
    hi = value.astype(jnp.bfloat16)
    rest = value - hi.astype(jnp.float32)
    mid = rest.astype(jnp.bfloat16)
    low = (rest - mid.astype(jnp.float32)).astype(jnp.bfloat16)
    lane = lax.broadcasted_iota(jnp.int32, (16, 256), 1)
    return jnp.where(lane == 0, hi, jnp.where(lane == 1, mid, jnp.where(lane == 2, low, jnp.bfloat16(0))))


def join3(rows):
    return jnp.sum(rows[0, :3].astype(jnp.float32))


def reduce_over(own, parts, total, axes, n):
    tail = split3(total)
    got = [send(jnp.concatenate([parts[s - 1], tail]), axes, s) for s in range(1, n)]
    acc = own.astype(jnp.float32)
    for g in got:
        acc = acc + g[:-16].astype(jnp.float32)
        total = total + join3(g[-16:])
    return acc.astype(jnp.bfloat16), total


def gather_over(piece, axes, n):
    return jnp.concatenate([piece] + [send(piece, axes, n - s) for s in range(1, n)])


def on_device(features, coords, quad_weight, mode_table, mode_weight, lin_weight, bias):
    width = features.shape[1]
    local_pts = features.shape[0]
    own_modes = mode_weight.shape[0]
    z, x, core = (lax.axis_index(a) for a in PTS)
    group = lax.axis_index(GRP)
    weighted = (quad_weight[:, None] * features.astype(jnp.float32)).astype(jnp.bfloat16)
    total = jnp.sum(quad_weight)
    grouped = mode_table.astype(jnp.float32).reshape(3, 4, 4, 2, 8, own_modes)
    wave = lax.dynamic_index_in_dim(grouped, group, 4, keepdims=False)
    wave = jnp.roll(wave, (-z, -x, -core), (1, 2, 3)).transpose(0, 3, 2, 1, 4).reshape(3, -1)
    modes = wave.shape[1]
    basis = phase_basis(coords, wave)
    term = lax.dot_general(
        basis, weighted, (((0,), (0,)), ((), ())), preferred_element_type=jnp.float32
    )
    term = jnp.concatenate([term[:modes], term[modes:]], axis=1).astype(jnp.bfloat16)
    half = modes // 2
    coef, total = reduce_over(term[:half], [term[half:]], total, ("core",), 2)
    q = half // 4
    coef, total = reduce_over(coef[:q], [coef[q * s : q * (s + 1)] for s in (1, 2, 3)], total, ("x",), 4)
    q = q // 4
    coef, total = reduce_over(coef[:q], [coef[q * s : q * (s + 1)] for s in (1, 2, 3)], total, ("z_hi",), 4)
    real_in = coef[:, :width]
    imag_in = coef[:, width:]
    w_real = mode_weight[:, 0]
    w_imag = mode_weight[:, 1]
    real_out = jnp.einsum(
        "mc,mcd->md", real_in, w_real, preferred_element_type=jnp.float32
    ) - jnp.einsum("mc,mcd->md", imag_in, w_imag, preferred_element_type=jnp.float32)
    imag_out = jnp.einsum(
        "mc,mcd->md", real_in, w_imag, preferred_element_type=jnp.float32
    ) + jnp.einsum("mc,mcd->md", imag_in, w_real, preferred_element_type=jnp.float32)
    filtered = jnp.concatenate([real_out, imag_out], axis=1).astype(jnp.bfloat16)
    piece = gather_over(filtered, ("z_hi",), 4)
    piece = gather_over(piece, ("x",), 4)
    piece = gather_over(piece, ("core",), 2)
    rhs = jnp.concatenate([piece[:, :width], piece[:, width:]], axis=0)
    field = jnp.dot(basis, rhs, preferred_element_type=jnp.float32).astype(jnp.bfloat16)
    out_rows = local_pts // 8
    blocks = field.reshape(8, out_rows, width)
    take = lambda a, i: lax.dynamic_index_in_dim(a, i, 0, keepdims=False)
    spectral = take(blocks, group).astype(jnp.float32)
    got = [send(take(blocks, lax.rem(group + s, 8)), GRP, s) for s in range(1, 8)]
    for g in got:
        spectral = spectral + g.astype(jnp.float32)
    my_features = lax.dynamic_slice_in_dim(features, group * out_rows, out_rows, 0)
    linear = jnp.dot(my_features, lin_weight, preferred_element_type=jnp.float32)
    pre = spectral / total + linear + bias[None, :]
    return jax.nn.gelu(pre, approximate=False).astype(jnp.bfloat16)


def solution(mesh):
    fine = Mesh(mesh.devices.reshape([SIZES[a] for a in ALL]), ALL)
    return jax.shard_map(
        on_device,
        mesh=fine,
        in_specs=(
            P(PTS, None),
            P(None, PTS),
            P(PTS),
            P(),
            P(ALL, None, None, None),
            P(),
            P(),
        ),
        out_specs=P(ALL, None),
        check_vma=False,
    )
```

```python
import functools
import math

import jax
import jax.numpy as jnp
from jax import lax
from jax.experimental import pallas as pl
from jax.experimental.pallas import tpu as pltpu
from jax.sharding import Mesh, PartitionSpec as P

SIZES = {"z_hi": 4, "x": 4, "core": 2, "y": 4, "z_lo": 2}
PTS = ("z_hi", "x", "core")
GRP = ("y", "z_lo")
ALL = PTS + GRP
C = 128
PITCH = C + 1
ROWS = 32
BF, F32 = jnp.bfloat16, jnp.float32
VM = pl.BlockSpec(memory_space=pltpu.VMEM)
SM = pl.BlockSpec(memory_space=pltpu.SMEM)


def call(body, n_in, out_shape, name, scratch=(), smem=0, flops=0, limit=None):
    many = isinstance(out_shape, (list, tuple))
    return pl.pallas_call(
        body,
        in_specs=[SM] * smem + [VM] * n_in,
        out_specs=[VM] * len(out_shape) if many else VM,
        out_shape=out_shape,
        scratch_shapes=list(scratch),
        compiler_params=pltpu.CompilerParams(vmem_limit_bytes=(limit or 16) * 2**20),
        cost_estimate=pl.CostEstimate(flops=flops, bytes_accessed=2**20, transcendentals=0),
        name=name,
    )


def send(value, axes, shift):
    n = 1
    for a in axes:
        n *= SIZES[a]
    return lax.ppermute(value, axes, [(j, (j + shift) % n) for j in range(n)])


def turn(x):
    h = math.pi * (x - jnp.round(x))
    q = h * h
    s = c = None
    for k in range(6, -1, -1):
        a = (-1) ** k / math.factorial(2 * k + 1)
        s = a if s is None else s * q + a
    for k in range(7, -1, -1):
        a = (-1) ** k / math.factorial(2 * k)
        c = a if c is None else c * q + a
    s = s * h
    return 1.0 - 2.0 * s * s, -2.0 * s * c


def times(a, b):
    return a[0] * b[0] - a[1] * b[1], a[0] * b[1] + a[1] * b[0]


def powers(x, n):
    one = turn(x)
    out = [(jnp.ones_like(x), jnp.zeros_like(x)), one]
    for k in range(2, n):
        out.append(times(out[k // 2], out[k - k // 2]))
    return out


def build_tables(coords, exy, ez, sl):
    for k, v in enumerate(powers(coords[2, sl], 32)):
        ez[k, 0, sl], ez[k, 1, sl] = v
    px, py = powers(coords[0, sl], 9), powers(coords[1, sl], 9)
    signed = lambda p, k: p[k] if k >= 0 else (p[-k][0], -p[-k][1])
    for kx in range(-8, 8):
        for ky in range(-8, 8):
            k = (kx + 8) * 16 + ky + 8
            exy[k, 0, sl], exy[k, 1, sl] = times(signed(px, kx), signed(py, ky))


def lanes3(value):
    hi = value.astype(BF).astype(F32)
    mid = (value - hi).astype(BF).astype(F32)
    low = value - hi - mid
    lane = lax.broadcasted_iota(jnp.int32, (16, C), 1)
    return jnp.where(lane == 0, hi, jnp.where(lane == 1, mid, jnp.where(lane == 2, low, 0.0))).astype(BF)


def total_of(rows):
    lane = lax.broadcasted_iota(jnp.int32, (1, C), 1)
    return jnp.sum(jnp.where(lane < 3, rows[:1], 0.0), axis=1, keepdims=True)


def analyse(flip, index, coef, basis, exy, ez, wt, total, scr):
    z, x, core = (lax.axis_index(a) for a in PTS)
    core = lax.rem(core + flip, 2)

    def block(dx):
        across = lax.rem(x + dx, 4)

        def some(it):
            own = (lax.rem(z + it // 2, 4) * 4 + across) * 2 + core
            for u in range(16):
                m = it * 16 + u
                k = index[own * 32 + lax.rem(it, 2) * 16 + u]
                ixy, iz = lax.shift_right_logical(k, 5), lax.bitwise_and(k, 31)
                for j in range(ROWS // 8):
                    sl = pl.ds(8 * j, 8)
                    re, im = times((exy[ixy, 0, sl], exy[ixy, 1, sl]), (ez[iz, 0, sl], ez[iz, 1, sl]))
                    scr[pl.ds(8 * j * PITCH + m, 8, stride=PITCH), :] = re
                    scr[pl.ds((ROWS + 8 * j) * PITCH + m, 8, stride=PITCH), :] = im

        pl.loop(0, C // 16)(some)
        at = pl.ds(pl.multiple_of(dx * C, C), C)
        acc = None
        for k in range(4):
            cols = pl.ds(k * 1024, 1024)
            both = []
            for part in range(2):
                rows = [scr[pl.ds((part * ROWS + k * 8 + h) * PITCH, C), :].astype(BF) for h in range(8)]
                both.append(jnp.concatenate(rows, axis=1))
                basis[part, at, cols] = both[-1]
            term = lax.dot_general(
                wt[:, cols], jnp.concatenate(both, axis=0), (((1,), (1,)), ((), ())), preferred_element_type=F32
            )
            acc = term if acc is None else acc + term
        coef[pl.ds(0, C), at] = acc[:, :C].astype(BF)
        coef[pl.ds(C, C), at] = acc[:, C:].astype(BF)
        coef[pl.ds(2 * C, 16), at] = lanes3(total)

    pl.loop(0, 4)(block)


def first_body(index, features, quad, coords, coef, basis, exy, ez, wt, scr):
    @pl.loop(0, ROWS)
    def _(o):
        at = pl.ds(pl.multiple_of(o * C, C), C)
        wt[:, at] = (features[at, :].astype(F32).T * quad[pl.ds(o, 1), :]).astype(BF)

    @pl.loop(0, ROWS // 8)
    def _(o):
        build_tables(coords, exy, ez, pl.ds(pl.multiple_of(8 * o, 8), 8))

    total = jnp.sum(jnp.sum(quad[...], axis=0, keepdims=True), axis=1, keepdims=True)
    analyse(1, index, coef, basis, exy, ez, wt, total, scr)


def second_body(index, quad, exy, ez, wt, coef, basis, scr):
    total = jnp.sum(jnp.sum(quad[...], axis=0, keepdims=True), axis=1, keepdims=True)
    analyse(0, index, coef, basis, exy, ez, wt, total, scr)


def pair_body(own, got, keep, out1, out2, out3):
    for s, ref in enumerate((keep, out1, out2, out3)):
        at = pl.ds(s * C, C)
        summed = own[pl.ds(0, 2 * C), at].astype(F32) + got[pl.ds(0, 2 * C), at].astype(F32)
        ref[pl.ds(0, 2 * C), :] = summed.astype(ref.dtype)
        tail = total_of(own[pl.ds(2 * C, 16), at].astype(F32) + got[pl.ds(2 * C, 16), at].astype(F32))
        ref[pl.ds(2 * C, 16), :] = lanes3(tail).astype(ref.dtype)


def across_body(own, got1, got2, got3, keep, out1, out2, out3):
    rows = pl.ds(2 * C, 16)
    tail = own[rows, :]
    for g in (got1, got2, got3):
        tail = tail + g[rows, :].astype(F32)
    tail = lanes3(total_of(tail))
    for part in range(2):
        rows = pl.ds(part * C, C)
        summed = own[rows, :]
        for g in (got1, got2, got3):
            summed = summed + g[rows, :].astype(F32)
        summed = summed.T
        for s, ref in enumerate((keep, out1, out2, out3)):
            ref[pl.ds(0, 32), pl.ds(part * C, C)] = summed[s * 32 : s * 32 + 32].astype(ref.dtype)
            ref[pl.ds(32, 16), pl.ds(part * C, C)] = tail.astype(ref.dtype)


def filter_body(own, got1, got2, got3, weight, out, total):
    summed = own[...]
    for g in (got1, got2, got3):
        summed = summed + g[...].astype(F32)
    total[...] = jnp.broadcast_to(total_of(summed[32:, :C]), total.shape)
    row = lax.rem(lax.broadcasted_iota(jnp.int32, (16, 2 * C), 0), 8)
    for g in range(4):
        block = summed[8 * g : 8 * g + 8]
        lhs = jnp.concatenate([block[:, :C], block[:, C:]], axis=0).astype(BF)
        picked = jnp.zeros((16, 2 * C), F32)
        for i in range(8):
            m = 8 * g + i
            both = jnp.concatenate([weight[m, 0], weight[m, 1]], axis=1)
            picked = jnp.where(row == i, jnp.dot(lhs, both, preferred_element_type=F32), picked)
        real = picked[:8, :C] - picked[8:, C:]
        imag = picked[:8, C:] + picked[8:, :C]
        out[pl.ds(8 * g, 8), :] = jnp.concatenate([real, imag], axis=1).astype(BF)


def turned_body(own, far, out0, out1):
    for src, out in ((own, out0), (far, out1)):
        for part in range(2):
            for s in range(4):
                block = src[pl.ds(s * C, C), pl.ds(part * C, C)].astype(F32).T
                out[:, pl.ds((part * 4 + s) * C, C)] = block.astype(BF)


def synthesis_body(shifts, own, far, basis0, basis1, *outs):
    group = lax.axis_index("y") * 2 + lax.axis_index("z_lo")
    for s, out in zip(shifts, outs, strict=True):
        at = pl.ds(pl.multiple_of(lax.rem(group + s, 8) * 512, 512), 512)
        acc = None
        for f, b in ((own, basis0), (far, basis1)):
            for part in range(2):
                term = jnp.dot(f[:, pl.ds(part * 512, 512)], b[part, :, at], preferred_element_type=F32)
                acc = term if acc is None else acc + term
        out[...] = acc.astype(BF)


def finish_body(total, features, lin, bias, *rest):
    *blocks, out = rest
    summed = blocks[0][...].astype(F32)
    for b in blocks[1:]:
        summed = summed + b[...].astype(F32)
    scaled = summed / total[0:1, 0:1]
    for k in range(4):
        rows = pl.ds(k * C, C)
        pre = scaled[:, k * C : k * C + C].T + jnp.dot(features[rows, :], lin[...], preferred_element_type=F32) + bias[...]
        out[rows, :] = (0.5 * pre * (1.0 + lax.erf(pre * math.sqrt(0.5)))).astype(BF)


def gather_over(piece, axes, n):
    return jnp.concatenate([piece] + [send(piece, axes, n - s) for s in range(1, n)])


def on_device(features, coords, quad_weight, mode_table, mode_weight, lin_weight, bias):
    pts = features.shape[0]
    group = lax.axis_index(GRP)
    table = mode_table.reshape(3, 32, 8, 32)
    table = lax.dynamic_index_in_dim(table, group, 2, keepdims=False)
    index = (((table[0] + 8) * 16 + table[1] + 8) * 32 + table[2]).reshape(1024)
    quad = quad_weight.reshape(ROWS, C)
    coords = coords.reshape(3, ROWS, C)
    scr = pltpu.VMEM((2 * ROWS * PITCH, C), F32)
    shape = jax.ShapeDtypeStruct
    coef_shape = shape((2 * C + 16, 512), BF)
    basis_shape = pltpu.VMEM((2, 512, pts), BF)
    half = 2 * 2 * 512 * pts * C
    far, basis1, exy, ez, wt = call(
        first_body, 3,
        [coef_shape, basis_shape, pltpu.VMEM((256, 2, ROWS, C), F32), pltpu.VMEM((32, 2, ROWS, C), F32), pltpu.VMEM((C, pts), BF)],
        "first_half", [scr], 1, 4 * half,
    )(index, features, quad, coords)
    near, basis0 = call(second_body, 4, [coef_shape, basis_shape], "second_half", [scr], 1, 3 * half)(
        index, quad, exy, ez, wt
    )
    got = send(far, ("core",), 1)
    one = lambda rows, cols, dt: shape((rows, cols), dt)
    keep, *outs = call(pair_body, 2, [one(272, C, F32)] + [one(272, C, BF)] * 3, "pair_sum")(near, got)
    got = [send(o, ("x",), s) for s, o in zip((1, 2, 3), outs)]
    keep, *outs = call(across_body, 4, [one(48, 2 * C, F32)] + [one(48, 2 * C, BF)] * 3, "x_sum")(keep, *got)
    got = [send(o, ("z_hi",), s) for s, o in zip((1, 2, 3), outs)]
    piece, total = call(filter_body, 5, [one(32, 2 * C, BF), one(8, C, F32)], "filter")(keep, *got, mode_weight)
    piece = gather_over(piece, ("z_hi",), 4)
    piece = gather_over(piece, ("x",), 4)
    other = send(piece, ("core",), 1)
    own, other = call(turned_body, 2, [one(C, 1024, BF)] * 2, "turned")(piece, other)
    fields = []
    for shifts in ((1, 2, 3), (4, 5), (6, 7), (0,)):
        out = [one(C, 512, BF)] * len(shifts)
        outs = call(functools.partial(synthesis_body, shifts), 4, out, "synthesis", flops=len(shifts) * half // 4)(
            own, other, basis0, basis1
        )
        fields += [send(o, GRP, s) if s else o for s, o in zip(shifts, outs)]
    rows = pts // 8
    mine = lax.dynamic_slice_in_dim(features, group * rows, rows, 0)
    return call(finish_body, 12, shape((rows, C), BF), "finish")(
        total, mine, lin_weight, bias.reshape(1, C), *fields
    )


def solution(mesh):
    fine = Mesh(mesh.devices.reshape([SIZES[a] for a in ALL]), ALL)
    return jax.shard_map(
        on_device,
        mesh=fine,
        in_specs=(
            P(PTS, None),
            P(None, PTS),
            P(PTS),
            P(),
            P(ALL, None, None, None),
            P(),
            P(),
        ),
        out_specs=P(ALL, None),
        check_vma=False,
    )
```

```python
import functools
import math

import jax
import jax.numpy as jnp
from jax import lax
from jax.experimental import pallas as pl
from jax.experimental.pallas import tpu as pltpu
from jax.sharding import Mesh, PartitionSpec as P

SIZES = {"z_hi": 4, "x": 4, "core": 2, "y": 4, "z_lo": 2}
PTS = ("z_hi", "x", "core")
GRP = ("y", "z_lo")
ALL = PTS + GRP
C = 128
PITCH = C + 1
ROWS = 32
BF, F32 = jnp.bfloat16, jnp.float32
VM = pl.BlockSpec(memory_space=pltpu.VMEM)
SM = pl.BlockSpec(memory_space=pltpu.SMEM)


def call(body, n_in, out_shape, name, scratch=(), smem=0, flops=0, aliases={}, last=(), room=16):
    many = isinstance(out_shape, (list, tuple))
    return pl.pallas_call(
        body,
        in_specs=[SM] * smem + [VM] * n_in + [pl.BlockSpec(memory_space=m) for m in last],
        out_specs=[VM] * len(out_shape) if many else VM,
        out_shape=out_shape,
        scratch_shapes=list(scratch),
        compiler_params=pltpu.CompilerParams(vmem_limit_bytes=room * 2**20),
        input_output_aliases=aliases,
        cost_estimate=pl.CostEstimate(flops=flops, bytes_accessed=2**20, transcendentals=0),
        name=name,
    )


def send(value, axes, shift):
    n = 1
    for a in axes:
        n *= SIZES[a]
    return lax.ppermute(value, axes, [(j, (j + shift) % n) for j in range(n)])


def turn(x):
    h = math.pi * (x - jnp.round(x))
    q = h * h
    s = c = None
    for k in range(6, -1, -1):
        a = (-1) ** k / math.factorial(2 * k + 1)
        s = a if s is None else s * q + a
    for k in range(7, -1, -1):
        a = (-1) ** k / math.factorial(2 * k)
        c = a if c is None else c * q + a
    s = s * h
    return 1.0 - 2.0 * s * s, -2.0 * s * c


def times(a, b):
    return a[0] * b[0] - a[1] * b[1], a[0] * b[1] + a[1] * b[0]


def powers(x, n):
    one = turn(x)
    out = [(jnp.ones_like(x), jnp.zeros_like(x)), one]
    for k in range(2, n):
        out.append(times(out[k // 2], out[k - k // 2]))
    return out


def build_tables(coords, exy, ez, sl):
    for k, v in enumerate(powers(coords[2], 32)):
        ez[k, 0, sl], ez[k, 1, sl] = v
    px, py = powers(coords[0], 9), powers(coords[1], 9)
    signed = lambda p, k: p[k] if k >= 0 else (p[-k][0], -p[-k][1])
    for kx in range(-8, 8):
        for ky in range(-8, 8):
            k = (kx + 8) * 16 + ky + 8
            exy[k, 0, sl], exy[k, 1, sl] = times(signed(px, kx), signed(py, ky))


def lanes3(value):
    hi = value.astype(BF).astype(F32)
    mid = (value - hi).astype(BF).astype(F32)
    low = value - hi - mid
    lane = lax.broadcasted_iota(jnp.int32, (16, C), 1)
    return jnp.where(lane == 0, hi, jnp.where(lane == 1, mid, jnp.where(lane == 2, low, 0.0))).astype(BF)


def total_of(rows):
    lane = lax.broadcasted_iota(jnp.int32, (1, C), 1)
    return jnp.sum(jnp.where(lane < 3, rows[:1], 0.0), axis=1, keepdims=True)


def analyse(flip, dz, index, put_coef, put_basis, exy, ez, wt, total, scr):
    z, x, core = (lax.axis_index(a) for a in PTS)
    start = lax.rem(z + dz, 4) * 8 + lax.rem(core + flip, 2)

    @pl.loop(0, C // 16)
    def _(it):
        own = start + lax.rem(x + it // 2, 4) * 2
        base = own * 32 + lax.rem(it, 2) * 16
        for u in range(16):
            m = it * 16 + u
            k = index[base + u]
            ixy, iz = lax.shift_right_logical(k, 5), lax.bitwise_and(k, 31)
            for j in range(ROWS // 8):
                sl = pl.ds(8 * j, 8)
                re, im = times((exy[ixy, 0, sl], exy[ixy, 1, sl]), (ez[iz, 0, sl], ez[iz, 1, sl]))
                scr[pl.ds(8 * j * PITCH + m, 8, stride=PITCH), :] = re
                scr[pl.ds((ROWS + 8 * j) * PITCH + m, 8, stride=PITCH), :] = im

    acc = None
    for k in range(4):
        cols = pl.ds(k * 1024, 1024)
        both = []
        for part in range(2):
            rows = [scr[pl.ds((part * ROWS + k * 8 + h) * PITCH, C), :].astype(BF) for h in range(8)]
            both.append(jnp.concatenate(rows, axis=1))
        both = jnp.concatenate(both, axis=0)
        put_basis(cols, both)
        term = lax.dot_general(wt[:, cols], both, (((1,), (1,)), ((), ())), preferred_element_type=F32)
        acc = term if acc is None else acc + term
    put_coef(jnp.concatenate([acc[:, :C].astype(BF), acc[:, C:].astype(BF), lanes3(total)], axis=0))


def sum_all(quad):
    return jnp.sum(jnp.sum(quad[...], axis=0, keepdims=True), axis=1, keepdims=True)


def first_body(index, *refs):
    given, (coef, basis, exy, ez, wt, linear, quad, scr), here, sems = refs[:5], refs[5:13], refs[13:17], refs[17]
    here = (here[0], quad, *here[1:])
    loads = [pltpu.make_async_copy(src, dst, sems.at[i]) for i, (src, dst) in enumerate(zip(given, here))]
    for load in loads:
        load.start()
    coords, quad, lin, bias, f = here
    loads[0].wait()

    @pl.loop(0, ROWS // 8)
    def _(o):
        row = lambda i, r: coords[pl.ds(i, 1), pl.ds(pl.multiple_of((8 * o + r) * C, C), C)]
        at = [jnp.concatenate([row(i, r) for r in range(8)], axis=0) for i in range(3)]
        build_tables(at, exy, ez, pl.ds(pl.multiple_of(8 * o, 8), 8))

    for load in loads[1:]:
        load.wait()
    same = lax.broadcasted_iota(jnp.int32, (C, C), 0) == lax.broadcasted_iota(jnp.int32, (C, C), 1)
    unit = jnp.where(same, 1.0, 0.0).astype(BF)
    for o in range(ROWS // 8):
        turned = lax.dot_general(
            unit, f[pl.ds(o * 8 * C, 8 * C), :], (((1,), (1,)), ((), ())), preferred_element_type=F32
        )
        for r in range(8):
            at = pl.ds((8 * o + r) * C, C)
            wt[:, at] = (turned[:, r * C : r * C + C] * quad[pl.ds(8 * o + r, 1), :]).astype(BF)
    group = lax.axis_index("y") * 2 + lax.axis_index("z_lo")
    mine = f[pl.ds(pl.multiple_of(group * 512, 512), 512), :]
    linear[...] = jnp.dot(mine, lin[...], preferred_element_type=F32) + bias[...]
    total = sum_all(quad)

    @pl.loop(0, 3)
    def _(s):
        def put_coef(value):
            coef[:, pl.ds(pl.multiple_of(s * C, C), C)] = value

        def put_basis(cols, value):
            basis[s, :, cols] = value

        analyse(1, s + 1, index, put_coef, put_basis, exy, ez, wt, total, scr)


def slab_body(flip, dz, index, quad, exy, ez, wt, after, coef, basis, scr):
    def put_coef(value):
        coef[...] = value

    def put_basis(cols, value):
        basis[:, cols] = value

    analyse(flip, dz, index, put_coef, put_basis, exy, ez, wt, sum_all(quad), scr)


def pair_body(s, own, got, out):
    at = pl.ds(s * C, C)
    summed = own[...].astype(F32) + got[:, at].astype(F32)
    out[pl.ds(0, 2 * C), :] = summed[: 2 * C].astype(BF)
    out[pl.ds(2 * C, 16), :] = lanes3(total_of(summed[2 * C :]))


def z_body(own, got0, got1, got2, got3, keep, out1, out2, out3):
    summed = own[...].astype(F32)
    for g in (got0, got1, got2, got3):
        summed = summed + g[...].astype(F32)
    tail = lanes3(total_of(summed[2 * C :]))
    for part in range(2):
        rows = summed[part * C : part * C + C].T
        for s, ref in enumerate((keep, out1, out2, out3)):
            ref[pl.ds(0, 32), pl.ds(part * C, C)] = rows[s * 32 : s * 32 + 32].astype(ref.dtype)
            ref[pl.ds(32, 16), pl.ds(part * C, C)] = tail.astype(ref.dtype)


def filter_body(own, got1, got2, got3, weight, out, total):
    summed = own[...]
    for g in (got1, got2, got3):
        summed = summed + g[...].astype(F32)
    total[...] = jnp.broadcast_to(total_of(summed[32:, :C]), total.shape)
    row = lax.rem(lax.broadcasted_iota(jnp.int32, (16, 2 * C), 0), 8)
    for g in range(4):
        block = summed[8 * g : 8 * g + 8]
        lhs = jnp.concatenate([block[:, :C], block[:, C:]], axis=0).astype(BF)
        picked = jnp.zeros((16, 2 * C), F32)
        for i in range(8):
            m = 8 * g + i
            both = jnp.concatenate([weight[m, 0], weight[m, 1]], axis=1)
            picked = jnp.where(row == i, jnp.dot(lhs, both, preferred_element_type=F32), picked)
        real = picked[:8, :C] - picked[8:, C:]
        imag = picked[:8, C:] + picked[8:, :C]
        out[pl.ds(8 * g, 8), :] = jnp.concatenate([real, imag], axis=1).astype(BF)


def turned_body(own, far, out):
    for flip, src in enumerate((own, far)):
        for dz in range(4):
            for part in range(2):
                cols = pl.ds(part * C, C)
                block = jnp.concatenate([src[pl.ds(dx * C + dz * 32, 32), cols].astype(F32) for dx in range(4)], axis=0)
                out[:, pl.ds(((flip * 4 + dz) * 2 + part) * C, C)] = block.T.astype(BF)


def synthesis_body(shifts, f, n0, n1, n2, n3, f0, f123, *outs):
    group = lax.axis_index("y") * 2 + lax.axis_index("z_lo")
    for s, out in zip(shifts, outs[: len(shifts)], strict=True):
        at = pl.ds(pl.multiple_of(lax.rem(group + s, 8) * 512, 512), 512)
        acc = None
        for i, b in enumerate((n0, n1, n2, n3, f0, f123.at[0], f123.at[1], f123.at[2])):
            term = jnp.dot(f[:, pl.ds(i * 2 * C, 2 * C)], b[:, at], preferred_element_type=F32)
            acc = term if acc is None else acc + term
        out[...] = acc.astype(BF)


def finish_body(total, linear, *rest):
    *blocks, out = rest
    summed = blocks[0][...].astype(F32)
    for b in blocks[1:]:
        summed = summed + b[...].astype(F32)
    scaled = summed / total[0:1, 0:1]
    for k in range(4):
        rows = pl.ds(k * C, C)
        pre = scaled[:, k * C : k * C + C].T + linear[rows, :]
        out[rows, :] = (0.5 * pre * (1.0 + lax.erf(pre * math.sqrt(0.5)))).astype(BF)


def gather_over(piece, axes, n):
    return jnp.concatenate([piece] + [send(piece, axes, n - s) for s in range(1, n)])


def on_device(features, coords, quad_weight, mode_table, mode_weight, lin_weight, bias):
    pts = features.shape[0]
    group = lax.axis_index(GRP)
    packed = ((mode_table[0] + 8) * 16 + mode_table[1] + 8) * 32 + mode_table[2]
    packed = lax.dynamic_index_in_dim(packed.reshape(32, 2, C), group // 4, 1, keepdims=False)
    index = lax.dynamic_slice_in_dim(packed, lax.rem(group, 4) * 32, 32, 1).reshape(1024)
    scr = pltpu.VMEM((2 * ROWS * PITCH, C), F32)
    one = lambda rows, cols, dt: jax.ShapeDtypeStruct((rows, cols), dt)
    tail = 2 * C + 16
    slab = 2 * 2 * C * pts * C
    far, f123, exy, ez, wt, linear, quad = call(
        first_body, 0,
        [pltpu.VMEM((tail, 3 * C), BF), pltpu.VMEM((3, 2 * C, pts), BF), pltpu.VMEM((256, 2, ROWS, C), F32),
         pltpu.VMEM((32, 2, ROWS, C), F32), pltpu.VMEM((C, pts), BF), pltpu.VMEM((pts // 8, C), F32), pltpu.VMEM((ROWS, C), F32)],
        "first",
        [scr, pltpu.VMEM((3, pts), F32), pltpu.VMEM((C, C), BF), pltpu.VMEM((1, C), F32), pltpu.VMEM((pts, C), BF),
         pltpu.SemaphoreType.DMA((5,))],
        1, 6 * slab, last=[pltpu.HBM] * 5, room=42,
    )(index, coords, quad_weight.reshape(ROWS, C), lin_weight, bias.reshape(1, C), features)
    got = send(far, ("core",), 1)

    def near(flip, dz, after):
        return call(
            functools.partial(slab_body, flip, dz), 4, [one(tail, C, BF), pltpu.VMEM((2 * C, pts), BF)],
            "slab", [scr], 1, 2 * slab, last=[pl.ANY],
        )(index, quad, exy, ez, wt, after)

    across, bases = {}, {}
    after = linear
    for dz in (2, 1, 3):
        mine, bases[dz] = near(0, dz, after)
        after = call(functools.partial(pair_body, dz - 1), 2, one(tail, C, BF), "pair")(mine, got)
        across[dz] = send(after, ("z_hi",), dz)
    far, f0 = near(1, 0, after)
    got = send(far, ("core",), 1)
    mine, bases[0] = near(0, 0, far)
    keep, *outs = call(z_body, 5, [one(48, 2 * C, F32)] + [one(48, 2 * C, BF)] * 3, "z_sum")(
        mine, got, across[1], across[2], across[3]
    )
    got = [send(o, ("x",), s) for s, o in zip((1, 2, 3), outs)]
    piece, total = call(filter_body, 5, [one(32, 2 * C, BF), one(8, C, F32)], "filter")(keep, *got, mode_weight)
    piece = gather_over(piece, ("z_hi",), 4)
    piece = gather_over(piece, ("x",), 4)
    other = send(piece, ("core",), 1)
    f = call(turned_body, 2, one(C, 2048, BF), "turned")(piece, other)
    fields = []
    bases = [bases[0], bases[1], bases[2], bases[3], f0, f123]
    for shifts in ((4, 3), (5, 2, 6), (1, 7, 0)):
        on = 0 not in shifts
        out = [one(C, 512, BF)] * len(shifts) + [pltpu.VMEM(b.shape, BF) for b in bases if on]
        outs = call(
            functools.partial(synthesis_body, shifts), 7, out, "synthesis", flops=len(shifts) * slab,
            aliases={i + 1: len(shifts) + i for i in range(6 if on else 0)},
        )(f, *bases)
        if on:
            bases = outs[len(shifts) :]
        fields += [send(o, GRP, s) if s else o for s, o in zip(shifts, outs)]
    return call(finish_body, 10, one(pts // 8, C, BF), "finish")(total, linear, *fields)


def solution(mesh):
    fine = Mesh(mesh.devices.reshape([SIZES[a] for a in ALL]), ALL)
    return jax.shard_map(
        on_device,
        mesh=fine,
        in_specs=(
            P(PTS, None),
            P(None, PTS),
            P(PTS),
            P(),
            P(ALL, None, None, None),
            P(),
            P(),
        ),
        out_specs=P(ALL, None),
        check_vma=False,
    )
```

```python
import functools
import math

import jax
import jax.numpy as jnp
from jax import lax
from jax.experimental import pallas as pl
from jax.experimental.pallas import tpu as pltpu
from jax.sharding import Mesh, PartitionSpec as P

SIZES = {"z_hi": 4, "x": 4, "core": 2, "y": 4, "z_lo": 2}
PTS = ("z_hi", "x", "core")
GRP = ("y", "z_lo")
ALL = PTS + GRP
C = 128
PITCH = C + 1
ROWS = 32
BF, F32 = jnp.bfloat16, jnp.float32
VM = pl.BlockSpec(memory_space=pltpu.VMEM)
SM = pl.BlockSpec(memory_space=pltpu.SMEM)


def call(body, n_in, out_shape, name, scratch=(), smem=0, flops=0, aliases={}, last=(), room=16):
    many = isinstance(out_shape, (list, tuple))
    return pl.pallas_call(
        body,
        in_specs=[SM] * smem + [VM] * n_in + [pl.BlockSpec(memory_space=m) for m in last],
        out_specs=[VM] * len(out_shape) if many else VM,
        out_shape=out_shape,
        scratch_shapes=list(scratch),
        compiler_params=pltpu.CompilerParams(vmem_limit_bytes=room * 2**20),
        input_output_aliases=aliases,
        cost_estimate=pl.CostEstimate(flops=flops, bytes_accessed=2**20, transcendentals=0),
        name=name,
    )


def send(value, axes, shift):
    n = 1
    for a in axes:
        n *= SIZES[a]
    return lax.ppermute(value, axes, [(j, (j + shift) % n) for j in range(n)])


def turn(x):
    h = math.pi * (x - jnp.round(x))
    q = h * h
    s = c = None
    for k in range(6, -1, -1):
        a = (-1) ** k / math.factorial(2 * k + 1)
        s = a if s is None else s * q + a
    for k in range(7, -1, -1):
        a = (-1) ** k / math.factorial(2 * k)
        c = a if c is None else c * q + a
    s = s * h
    return 1.0 - 2.0 * s * s, -2.0 * s * c


def times(a, b):
    return a[0] * b[0] - a[1] * b[1], a[0] * b[1] + a[1] * b[0]


def powers(x, n):
    one = turn(x)
    out = [(jnp.ones_like(x), jnp.zeros_like(x)), one]
    for k in range(2, n):
        out.append(times(out[k // 2], out[k - k // 2]))
    return out


def build_tables(coords, exy, ez, sl):
    for k, v in enumerate(powers(coords[2], 32)):
        ez[k, 0, sl], ez[k, 1, sl] = v
    px, py = powers(coords[0], 9), powers(coords[1], 9)
    signed = lambda p, k: p[k] if k >= 0 else (p[-k][0], -p[-k][1])
    for kx in range(-8, 8):
        for ky in range(-8, 8):
            k = (kx + 8) * 16 + ky + 8
            exy[k, 0, sl], exy[k, 1, sl] = times(signed(px, kx), signed(py, ky))


def lanes3(value):
    hi = value.astype(BF).astype(F32)
    mid = (value - hi).astype(BF).astype(F32)
    low = value - hi - mid
    lane = lax.broadcasted_iota(jnp.int32, (16, C), 1)
    return jnp.where(lane == 0, hi, jnp.where(lane == 1, mid, jnp.where(lane == 2, low, 0.0))).astype(BF)


def total_of(rows):
    lane = lax.broadcasted_iota(jnp.int32, (1, C), 1)
    return jnp.sum(jnp.where(lane < 3, rows[:1], 0.0), axis=1, keepdims=True)


def analyse(index, row, put_coef, put_basis, exy, ez, w, scr):
    @pl.loop(0, C // 16)
    def _(it):
        for u in range(16):
            m = it * 16 + u
            k = index[row, m]
            ixy, iz = lax.shift_right_logical(k, 5), lax.bitwise_and(k, 31)
            for j in range(ROWS // 8):
                sl = pl.ds(8 * j, 8)
                re, im = times((exy[ixy, 0, sl], exy[ixy, 1, sl]), (ez[iz, 0, sl], ez[iz, 1, sl]))
                scr[pl.ds(8 * j * PITCH + m, 8, stride=PITCH), :] = re
                scr[pl.ds((ROWS + 8 * j) * PITCH + m, 8, stride=PITCH), :] = im

    acc = None
    for k in range(4):
        cols = pl.ds(k * 1024, 1024)
        both = []
        for part in range(2):
            rows = [scr[pl.ds((part * ROWS + k * 8 + h) * PITCH, C), :].astype(BF) for h in range(8)]
            both.append(jnp.concatenate(rows, axis=1))
        both = jnp.concatenate(both, axis=0)
        put_basis(cols, both)
        term = jnp.dot(both, w[cols, :], preferred_element_type=F32)
        acc = term if acc is None else acc + term
    put_coef(acc.astype(BF))


def slabs(count, first, index, coef, basis, exy, ez, w, quad, scr):
    @pl.loop(0, count)
    def _(s):
        def put_coef(value):
            coef[pl.ds(pl.multiple_of(s * 2 * C, 2 * C), 2 * C), :] = value

        def put_basis(cols, value):
            basis[s, :, cols] = value

        analyse(index, first + s, put_coef, put_basis, exy, ez, w, scr)

    total = jnp.sum(jnp.sum(quad[...], axis=0, keepdims=True), axis=1, keepdims=True)
    coef[pl.ds(count * 2 * C, 16), :] = lanes3(total)


def pack_index(table, index):
    z, x, core = (lax.axis_index(a) for a in PTS)
    group = lax.axis_index("y") * 2 + lax.axis_index("z_lo")
    tile, within = group // 4, lax.rem(group, 4)
    part = lax.broadcasted_iota(jnp.int32, (1, C), 1) // 32
    for flip in range(2):
        for dz in range(4):
            row = jnp.zeros((1, C), jnp.int32)
            for dx in range(4):
                own = (lax.rem(z + dz, 4) * 4 + lax.rem(x + dx, 4)) * 2 + lax.rem(core + flip, 2)
                v = table[:, pl.ds(pl.multiple_of(own * 256 + tile * C, C), C)]
                k = ((v[0:1] + 8) * 16 + v[1:2] + 8) * 32 + v[2:3]
                k = pltpu.roll(k, lax.rem(dx - within + 4, 4) * 32, 1)
                row = jnp.where(part == dx, k, row)
            index[pl.ds(flip * 4 + dz, 1), :] = row


def first_body(*refs):
    given, (coef, basis, exy, ez, w, linear, quad, index) = refs[:6], refs[6:14]
    scr, coords, table, lin, bias, f, held, sems = refs[14:]
    here = (coords, table, quad, lin, bias, f)
    loads = [pltpu.make_async_copy(src, dst, sems.at[i]) for i, (src, dst) in enumerate(zip(given, here))]
    for load in loads:
        load.start()
    loads[0].wait()

    @pl.loop(0, ROWS // 8)
    def _(o):
        row = lambda i, r: coords[pl.ds(i, 1), pl.ds(pl.multiple_of((8 * o + r) * C, C), C)]
        at = [jnp.concatenate([row(i, r) for r in range(8)], axis=0) for i in range(3)]
        build_tables(at, exy, ez, pl.ds(pl.multiple_of(8 * o, 8), 8))

    loads[1].wait()
    pack_index(table, index)
    hold = pltpu.make_async_copy(index, held, sems.at[6])
    hold.start()
    for load in loads[2:]:
        load.wait()
    columns = quad[...].T
    for o in range(ROWS):
        rows = pl.ds(o * C, C)
        w[rows, :] = (f[rows, :].astype(F32) * columns[:, o : o + 1]).astype(BF)
    group = lax.axis_index("y") * 2 + lax.axis_index("z_lo")
    mine = f[pl.ds(pl.multiple_of(group * 512, 512), 512), :]
    linear[...] = jnp.dot(mine, lin[...], preferred_element_type=F32) + bias[...]
    hold.wait()
    slabs(4, 4, held, coef, basis, exy, ez, w, quad, scr)


def near_body(count, first, index, quad, exy, ez, w, after, coef, basis, scr):
    slabs(count, first, index, coef, basis, exy, ez, w, quad, scr)


def pair_body(own, got, *outs):
    tail = total_of(own[pl.ds(6 * C, 16), :].astype(F32) + got[pl.ds(8 * C, 16), :].astype(F32))
    for s, out in enumerate(outs):
        summed = own[pl.ds(s * 2 * C, 2 * C), :].astype(F32) + got[pl.ds((s + 1) * 2 * C, 2 * C), :].astype(F32)
        out[pl.ds(0, 2 * C), :] = summed.astype(BF)
        out[pl.ds(2 * C, 16), :] = lanes3(tail)


def z_body(own, got0, got1, got2, got3, keep, out1, out2, out3):
    body, rest = pl.ds(0, 2 * C), pl.ds(2 * C, 16)
    summed = own[body, :].astype(F32) + got0[body, :].astype(F32)
    tail = own[rest, :].astype(F32) + got0[pl.ds(8 * C, 16), :].astype(F32)
    for g in (got1, got2, got3):
        summed = summed + g[body, :].astype(F32)
        tail = tail + g[rest, :].astype(F32)
    tail = lanes3(total_of(tail))
    for part in range(2):
        cols = pl.ds(part * C, C)
        for s, ref in enumerate((keep, out1, out2, out3)):
            at = part * C + s * 32
            ref[pl.ds(0, 32), cols] = summed[at : at + 32].astype(ref.dtype)
            ref[pl.ds(32, 16), cols] = tail.astype(ref.dtype)


def filter_body(own, got1, got2, got3, weight, out, total):
    summed = own[...]
    for g in (got1, got2, got3):
        summed = summed + g[...].astype(F32)
    total[...] = jnp.broadcast_to(total_of(summed[32:, :C]), total.shape)
    row = lax.rem(lax.broadcasted_iota(jnp.int32, (16, 2 * C), 0), 8)
    for g in range(4):
        block = summed[8 * g : 8 * g + 8]
        lhs = jnp.concatenate([block[:, :C], block[:, C:]], axis=0).astype(BF)
        picked = jnp.zeros((16, 2 * C), F32)
        for i in range(8):
            m = 8 * g + i
            both = jnp.concatenate([weight[m, 0], weight[m, 1]], axis=1)
            picked = jnp.where(row == i, jnp.dot(lhs, both, preferred_element_type=F32), picked)
        real = picked[:8, :C] - picked[8:, C:]
        imag = picked[:8, C:] + picked[8:, :C]
        out[pl.ds(8 * g, 8), :] = jnp.concatenate([real, imag], axis=1).astype(BF)


def turned_body(src, out):
    for dz in range(4):
        for part in range(2):
            cols = pl.ds(part * C, C)
            block = jnp.concatenate([src[pl.ds(dx * C + dz * 32, 32), cols].astype(F32) for dx in range(4)], axis=0)
            out[:, pl.ds((dz * 2 + part) * C, C)] = block.T.astype(BF)


def near_field_body(src, n0, n123, part, f):
    turned_body(src, f)

    @pl.loop(0, 8)
    def _(k):
        at = pl.ds(pl.multiple_of(k * 512, 512), 512)
        acc = None
        for i, b in enumerate((n0.at[0], n123.at[0], n123.at[1], n123.at[2])):
            term = jnp.dot(f[:, pl.ds(i * 2 * C, 2 * C)], b[:, at], preferred_element_type=F32)
            acc = term if acc is None else acc + term
        part[:, at] = acc


def synthesis_body(shifts, f, basis, part, *outs):
    group = lax.axis_index("y") * 2 + lax.axis_index("z_lo")
    for s, out in zip(shifts, outs[: len(shifts)], strict=True):
        at = pl.ds(pl.multiple_of(lax.rem(group + s, 8) * 512, 512), 512)
        acc = part[:, at]
        for i in range(4):
            acc = acc + jnp.dot(f[:, pl.ds(i * 2 * C, 2 * C)], basis[i, :, at], preferred_element_type=F32)
        out[...] = acc.astype(BF)


def finish_body(total, linear, *rest):
    *blocks, out = rest
    summed = blocks[0][...].astype(F32)
    for b in blocks[1:]:
        summed = summed + b[...].astype(F32)
    scaled = summed / total[0:1, 0:1]
    for k in range(4):
        rows = pl.ds(k * C, C)
        pre = scaled[:, k * C : k * C + C].T + linear[rows, :]
        out[rows, :] = (0.5 * pre * (1.0 + lax.erf(pre * math.sqrt(0.5)))).astype(BF)


def gather_over(piece, axes, n):
    return jnp.concatenate([piece] + [send(piece, axes, n - s) for s in range(1, n)])


def on_device(features, coords, quad_weight, mode_table, mode_weight, lin_weight, bias):
    pts = features.shape[0]
    scr = pltpu.VMEM((2 * ROWS * PITCH, C), F32)
    one = lambda rows, cols, dt: jax.ShapeDtypeStruct((rows, cols), dt)
    slab = 2 * 2 * C * pts * C
    far, far_basis, exy, ez, w, linear, quad, index = call(
        first_body, 0,
        [pltpu.VMEM((8 * C + 16, C), BF), pltpu.VMEM((4, 2 * C, pts), BF), pltpu.VMEM((256, 2, ROWS, C), F32),
         pltpu.VMEM((32, 2, ROWS, C), F32), pltpu.VMEM((pts, C), BF), pltpu.VMEM((pts // 8, C), F32),
         pltpu.VMEM((ROWS, C), F32), pltpu.VMEM((8, C), jnp.int32)],
        "first",
        [scr, pltpu.VMEM((3, pts), F32), pltpu.VMEM((3, 8192), jnp.int32), pltpu.VMEM((C, C), BF), pltpu.VMEM((1, C), F32),
         pltpu.VMEM((pts, C), BF), pltpu.SMEM((8, C), jnp.int32), pltpu.SemaphoreType.DMA((7,))],
        0, 8 * slab, last=[pltpu.HBM] * 6, room=42,
    )(coords, mode_table, quad_weight.reshape(ROWS, C), lin_weight, bias.reshape(1, C), features)
    got = send(far, ("core",), 1)

    def near(count, first, after):
        return call(
            functools.partial(near_body, count, first), 4,
            [pltpu.VMEM((count * 2 * C + 16, C), BF), pltpu.VMEM((count, 2 * C, pts), BF)],
            "near", [scr], 1, 2 * count * slab, last=[pl.ANY],
        )(index, quad, exy, ez, w, after)

    mine, n123 = near(3, 1, linear)
    outs = call(pair_body, 2, [one(2 * C + 16, C, BF)] * 3, "pair")(mine, got)
    across = {s: send(outs[s - 1], ("z_hi",), s) for s in (2, 1, 3)}
    mine, n0 = near(1, 0, outs[0])
    keep, *outs = call(z_body, 5, [one(48, 2 * C, F32)] + [one(48, 2 * C, BF)] * 3, "z_sum")(
        mine, got, across[1], across[2], across[3]
    )
    got = [send(o, ("x",), s) for s, o in zip((1, 2, 3), outs)]
    piece, total = call(filter_body, 5, [one(32, 2 * C, BF), one(8, C, F32)], "filter")(keep, *got, mode_weight)
    piece = gather_over(piece, ("z_hi",), 4)
    piece = gather_over(piece, ("x",), 4)
    other = send(piece, ("core",), 1)
    part = call(
        near_field_body, 3, pltpu.VMEM((C, pts), F32), "near_field", [pltpu.VMEM((C, 8 * C), BF)], flops=4 * slab
    )(piece, n0, n123)
    f = call(turned_body, 1, one(C, 8 * C, BF), "turned")(other)
    fields = []
    for shifts in ((4, 3), (5, 2, 6), (1, 7, 0)):
        count = len(shifts)
        chain = [pltpu.VMEM(v.shape, v.dtype) for v in (far_basis, part)] if 0 not in shifts else []
        outs = call(
            functools.partial(synthesis_body, shifts), 3, [one(C, 512, BF)] * count + chain, "synthesis",
            flops=count * slab // 2, aliases={1: count, 2: count + 1} if chain else {},
        )(f, far_basis, part)
        if chain:
            far_basis, part = outs[count:]
        fields += [send(o, GRP, s) if s else o for s, o in zip(shifts, outs)]
    return call(finish_body, 10, one(pts // 8, C, BF), "finish")(total, linear, *fields)


def solution(mesh):
    fine = Mesh(mesh.devices.reshape([SIZES[a] for a in ALL]), ALL)
    return jax.shard_map(
        on_device,
        mesh=fine,
        in_specs=(
            P(PTS, None),
            P(None, PTS),
            P(PTS),
            P(),
            P(ALL, None, None, None),
            P(),
            P(),
        ),
        out_specs=P(ALL, None),
        check_vma=False,
    )
```

```python
import functools
import math

import jax
import jax.numpy as jnp
from jax import lax
from jax.experimental import pallas as pl
from jax.experimental.pallas import tpu as pltpu
from jax.sharding import Mesh, PartitionSpec as P

SIZES = {"z_hi": 4, "x": 4, "core": 2, "y": 4, "z_lo": 2}
PTS = ("z_hi", "x", "core")
GRP = ("y", "z_lo")
ALL = PTS + GRP
FAR_LAST = (1, 3, 2)
C = 128
PITCH = C + 1
ROWS = 32
BF, F32 = jnp.bfloat16, jnp.float32
VM = pl.BlockSpec(memory_space=pltpu.VMEM)
SM = pl.BlockSpec(memory_space=pltpu.SMEM)


def call(body, n_in, out_shape, name, scratch=(), smem=0, flops=0, aliases={}, last=(), room=16):
    many = isinstance(out_shape, (list, tuple))
    return pl.pallas_call(
        body,
        in_specs=[SM] * smem + [VM] * n_in + [pl.BlockSpec(memory_space=m) for m in last],
        out_specs=[VM] * len(out_shape) if many else VM,
        out_shape=out_shape,
        scratch_shapes=list(scratch),
        compiler_params=pltpu.CompilerParams(vmem_limit_bytes=room * 2**20),
        input_output_aliases=aliases,
        cost_estimate=pl.CostEstimate(flops=flops, bytes_accessed=2**20, transcendentals=0),
        name=name,
    )


def send(value, axes, shift):
    n = 1
    for a in axes:
        n *= SIZES[a]
    return lax.ppermute(value, axes, [(j, (j + shift) % n) for j in range(n)])


def turn(x):
    h = math.pi * (x - jnp.round(x))
    q = h * h
    s = c = None
    for k in range(6, -1, -1):
        a = (-1) ** k / math.factorial(2 * k + 1)
        s = a if s is None else s * q + a
    for k in range(7, -1, -1):
        a = (-1) ** k / math.factorial(2 * k)
        c = a if c is None else c * q + a
    s = s * h
    return 1.0 - 2.0 * s * s, -2.0 * s * c


def times(a, b):
    return a[0] * b[0] - a[1] * b[1], a[0] * b[1] + a[1] * b[0]


def powers(x, n):
    one = turn(x)
    out = [(jnp.ones_like(x), jnp.zeros_like(x)), one]
    for k in range(2, n):
        out.append(times(out[k // 2], out[k - k // 2]))
    return out


def build_tables(coords, exy, ez, sl):
    for k, v in enumerate(powers(coords[2], 32)):
        ez[k, 0, sl], ez[k, 1, sl] = v
    px, py = powers(coords[0], 9), powers(coords[1], 9)
    signed = lambda p, k: p[k] if k >= 0 else (p[-k][0], -p[-k][1])
    for kx in range(-8, 8):
        for ky in range(-8, 8):
            k = (kx + 8) * 16 + ky + 8
            exy[k, 0, sl], exy[k, 1, sl] = times(signed(px, kx), signed(py, ky))


def lanes3(value):
    hi = value.astype(BF).astype(F32)
    mid = (value - hi).astype(BF).astype(F32)
    low = value - hi - mid
    lane = lax.broadcasted_iota(jnp.int32, (16, C), 1)
    return jnp.where(lane == 0, hi, jnp.where(lane == 1, mid, jnp.where(lane == 2, low, 0.0))).astype(BF)


def total_of(rows):
    lane = lax.broadcasted_iota(jnp.int32, (1, C), 1)
    return jnp.sum(jnp.where(lane < 3, rows[:1], 0.0), axis=1, keepdims=True)


def analyse(index, row, put_coef, put_basis, exy, ez, w, scr):
    @pl.loop(0, C // 16)
    def _(it):
        for u in range(16):
            m = it * 16 + u
            k = index[row, m]
            ixy, iz = lax.shift_right_logical(k, 5), lax.bitwise_and(k, 31)
            for j in range(ROWS // 8):
                sl = pl.ds(8 * j, 8)
                re, im = times((exy[ixy, 0, sl], exy[ixy, 1, sl]), (ez[iz, 0, sl], ez[iz, 1, sl]))
                scr[pl.ds(8 * j * PITCH + m, 8, stride=PITCH), :] = re
                scr[pl.ds((ROWS + 8 * j) * PITCH + m, 8, stride=PITCH), :] = im

    acc = None
    for k in range(4):
        cols = pl.ds(k * 1024, 1024)
        both = []
        for part in range(2):
            rows = [scr[pl.ds((part * ROWS + k * 8 + h) * PITCH, C), :].astype(BF) for h in range(8)]
            both.append(jnp.concatenate(rows, axis=1))
        both = jnp.concatenate(both, axis=0)
        put_basis(cols, both)
        term = jnp.dot(both, w[cols, :], preferred_element_type=F32)
        acc = term if acc is None else acc + term
    put_coef(acc.astype(BF))


def slabs(count, first, index, coef, basis, exy, ez, w, quad, scr):
    @pl.loop(0, count)
    def _(s):
        def put_coef(value):
            coef[pl.ds(pl.multiple_of(s * 2 * C, 2 * C), 2 * C), :] = value

        def put_basis(cols, value):
            basis[pl.ds(pl.multiple_of((first % 4 + s) * 2 * C, 2 * C), 2 * C), cols] = value

        analyse(index, first + s, put_coef, put_basis, exy, ez, w, scr)

    total = jnp.sum(jnp.sum(quad[...], axis=0, keepdims=True), axis=1, keepdims=True)
    coef[pl.ds(count * 2 * C, 16), :] = lanes3(total)


def pack_index(table, index):
    z, x, core = (lax.axis_index(a) for a in PTS)
    group = lax.axis_index("y") * 2 + lax.axis_index("z_lo")
    tile, within = group // 4, lax.rem(group, 4)
    part = lax.broadcasted_iota(jnp.int32, (1, C), 1) // 32
    for flip in range(2):
        for dx in range(4):
            row = jnp.zeros((1, C), jnp.int32)
            for dz in range(4):
                own = (lax.rem(z + dz, 4) * 4 + lax.rem(x + dx, 4)) * 2 + lax.rem(core + flip, 2)
                v = table[:, pl.ds(pl.multiple_of(own * 256 + tile * C, C), C)]
                k = ((v[0:1] + 8) * 16 + v[1:2] + 8) * 32 + v[2:3]
                k = pltpu.roll(k, lax.rem(dz - within + 4, 4) * 32, 1)
                row = jnp.where(part == dz, k, row)
            index[pl.ds(flip * 4 + dx, 1), :] = row


def first_body(*refs):
    given, (coef, basis, exy, ez, w, linear, quad, index) = refs[:6], refs[6:14]
    scr, coords, table, lin, bias, f, held, sems = refs[14:]
    here = (coords, table, quad, lin, bias, f)
    loads = [pltpu.make_async_copy(src, dst, sems.at[i]) for i, (src, dst) in enumerate(zip(given, here))]
    for load in loads:
        load.start()
    loads[0].wait()

    @pl.loop(0, ROWS // 8)
    def _(o):
        row = lambda i, r: coords[pl.ds(i, 1), pl.ds(pl.multiple_of((8 * o + r) * C, C), C)]
        at = [jnp.concatenate([row(i, r) for r in range(8)], axis=0) for i in range(3)]
        build_tables(at, exy, ez, pl.ds(pl.multiple_of(8 * o, 8), 8))

    loads[1].wait()
    pack_index(table, index)
    hold = pltpu.make_async_copy(index, held, sems.at[6])
    hold.start()
    for load in loads[2:]:
        load.wait()
    columns = quad[...].T
    for o in range(ROWS):
        rows = pl.ds(o * C, C)
        w[rows, :] = (f[rows, :].astype(F32) * columns[:, o : o + 1]).astype(BF)
    group = lax.axis_index("y") * 2 + lax.axis_index("z_lo")
    mine = f[pl.ds(pl.multiple_of(group * 512, 512), 512), :]
    linear[...] = jnp.dot(mine, lin[...], preferred_element_type=F32) + bias[...]
    hold.wait()
    slabs(4, 4, held, coef, basis, exy, ez, w, quad, scr)


def near_body(count, first, index, quad, exy, ez, w, given, coef, basis, scr):
    slabs(count, first, index, coef, basis, exy, ez, w, quad, scr)


def pair_body(own, got, *outs):
    tail = total_of(own[pl.ds(6 * C, 16), :].astype(F32) + got[pl.ds(8 * C, 16), :].astype(F32))
    for s, out in enumerate(outs):
        summed = own[pl.ds(s * 2 * C, 2 * C), :].astype(F32) + got[pl.ds((s + 1) * 2 * C, 2 * C), :].astype(F32)
        out[pl.ds(0, 2 * C), :] = summed.astype(BF)
        out[pl.ds(2 * C, 16), :] = lanes3(tail)


def x_body(own, got0, got1, got2, got3, keep, out1, out2, out3):
    body, rest = pl.ds(0, 2 * C), pl.ds(2 * C, 16)
    summed = own[body, :].astype(F32) + got0[body, :].astype(F32)
    tail = own[rest, :].astype(F32) + got0[pl.ds(8 * C, 16), :].astype(F32)
    for g in (got1, got2, got3):
        summed = summed + g[body, :].astype(F32)
        tail = tail + g[rest, :].astype(F32)
    tail = lanes3(total_of(tail))
    for part in range(2):
        cols = pl.ds(part * C, C)
        for s, ref in enumerate((keep, out1, out2, out3)):
            at = part * C + s * 32
            ref[pl.ds(0, 32), cols] = summed[at : at + 32].astype(ref.dtype)
            ref[pl.ds(32, 16), cols] = tail.astype(ref.dtype)


def filter_body(own, got1, got2, got3, weight, out, total):
    summed = own[...]
    for g in (got1, got2, got3):
        summed = summed + g[...].astype(F32)
    total[...] = jnp.broadcast_to(total_of(summed[32:, :C]), total.shape)
    row = lax.rem(lax.broadcasted_iota(jnp.int32, (16, 2 * C), 0), 8)
    for g in range(4):
        block = summed[8 * g : 8 * g + 8]
        lhs = jnp.concatenate([block[:, :C], block[:, C:]], axis=0).astype(BF)
        picked = jnp.zeros((16, 2 * C), F32)
        for i in range(8):
            m = 8 * g + i
            both = jnp.concatenate([weight[m, 0], weight[m, 1]], axis=1)
            picked = jnp.where(row == i, jnp.dot(lhs, both, preferred_element_type=F32), picked)
        real = picked[:8, :C] - picked[8:, C:]
        imag = picked[:8, C:] + picked[8:, :C]
        out[pl.ds(8 * g, 8), :] = jnp.concatenate([real, imag], axis=1).astype(BF)


def turned_body(src, out):
    for dx in range(4):
        for part in range(2):
            block = src[pl.ds(dx * C, C), pl.ds(part * C, C)].astype(F32).T
            out[:, pl.ds((dx * 2 + part) * C, C)] = block.astype(BF)


def near_field_body(src, basis, part, f):
    turned_body(src, f)

    @pl.loop(0, 8)
    def _(k):
        at = pl.ds(pl.multiple_of(k * 512, 512), 512)
        part[:, at] = jnp.dot(f[...], basis[:, at], preferred_element_type=F32)


def synthesis_body(shifts, f, basis, part, *outs):
    group = lax.axis_index("y") * 2 + lax.axis_index("z_lo")
    for s, out in zip(shifts, outs[: len(shifts)], strict=True):
        at = pl.ds(pl.multiple_of(lax.rem(group + s, 8) * 512, 512), 512)
        out[...] = (part[:, at] + jnp.dot(f[...], basis[:, at], preferred_element_type=F32)).astype(BF)


def finish_body(total, linear, *rest):
    *blocks, out = rest
    summed = blocks[0][...].astype(F32)
    for b in blocks[1:]:
        summed = summed + b[...].astype(F32)
    scaled = summed / total[0:1, 0:1]
    for k in range(4):
        rows = pl.ds(k * C, C)
        pre = scaled[:, k * C : k * C + C].T + linear[rows, :]
        out[rows, :] = (0.5 * pre * (1.0 + lax.erf(pre * math.sqrt(0.5)))).astype(BF)


def join_body(piece, *rest):
    *got, out = rest
    rows = piece.shape[0]
    for s, ref in zip((0, *FAR_LAST), (piece, *got)):
        out[pl.ds(s * rows, rows), :] = ref[...]


def gather_over(piece, axes, n):
    got = [send(piece, axes, n - s) for s in FAR_LAST]
    shape = jax.ShapeDtypeStruct((n * piece.shape[0], piece.shape[1]), piece.dtype)
    return call(join_body, n, shape, "join")(piece, *got)


def on_device(features, coords, quad_weight, mode_table, mode_weight, lin_weight, bias):
    pts = features.shape[0]
    scr = pltpu.VMEM((2 * ROWS * PITCH, C), F32)
    one = lambda rows, cols, dt: jax.ShapeDtypeStruct((rows, cols), dt)
    slab = 2 * 2 * C * pts * C
    far, far_basis, exy, ez, w, linear, quad, index = call(
        first_body, 0,
        [pltpu.VMEM((8 * C + 16, C), BF), pltpu.VMEM((8 * C, pts), BF), pltpu.VMEM((256, 2, ROWS, C), F32),
         pltpu.VMEM((32, 2, ROWS, C), F32), pltpu.VMEM((pts, C), BF), pltpu.VMEM((pts // 8, C), F32),
         pltpu.VMEM((ROWS, C), F32), pltpu.VMEM((8, C), jnp.int32)],
        "first",
        [scr, pltpu.VMEM((3, pts), F32), pltpu.VMEM((3, 8192), jnp.int32), pltpu.VMEM((C, C), BF), pltpu.VMEM((1, C), F32),
         pltpu.VMEM((pts, C), BF), pltpu.SMEM((8, C), jnp.int32), pltpu.SemaphoreType.DMA((7,))],
        0, 8 * slab, last=[pltpu.HBM] * 6, room=42,
    )(coords, mode_table, quad_weight.reshape(ROWS, C), lin_weight, bias.reshape(1, C), features)
    got = send(far, ("core",), 1)

    def near(count, first, given, alias):
        return call(
            functools.partial(near_body, count, first), 4,
            [pltpu.VMEM((count * 2 * C + 16, C), BF), pltpu.VMEM((8 * C, pts), BF)],
            "near", [scr], 1, 2 * count * slab, last=[pltpu.VMEM if alias else pl.ANY], aliases={5: 1} if alias else {},
        )(index, quad, exy, ez, w, given)

    mine, basis = near(3, 1, linear, False)
    outs = call(pair_body, 2, [one(2 * C + 16, C, BF)] * 3, "pair")(mine, got)
    across = {s: send(outs[s - 1], ("x",), s) for s in FAR_LAST}
    mine, basis = near(1, 0, basis, True)
    keep, *outs = call(x_body, 5, [one(48, 2 * C, F32)] + [one(48, 2 * C, BF)] * 3, "x_sum")(
        mine, got, *[across[s] for s in FAR_LAST]
    )
    got = [send(outs[s - 1], ("z_hi",), s) for s in FAR_LAST]
    piece, total = call(filter_body, 5, [one(32, 2 * C, BF), one(8, C, F32)], "filter")(keep, *got, mode_weight)
    piece = gather_over(piece, ("z_hi",), 4)
    piece = gather_over(piece, ("x",), 4)
    other = send(piece, ("core",), 1)
    part = call(
        near_field_body, 2, pltpu.VMEM((C, pts), F32), "near_field", [pltpu.VMEM((C, 8 * C), BF)], flops=4 * slab
    )(piece, basis)
    f = call(turned_body, 1, one(C, 8 * C, BF), "turned")(other)
    fields = []
    for shifts in ((4, 3), (5, 2, 6), (1, 7, 0)):
        count = len(shifts)
        chain = [pltpu.VMEM(v.shape, v.dtype) for v in (far_basis, part)] if 0 not in shifts else []
        outs = call(
            functools.partial(synthesis_body, shifts), 3, [one(C, 512, BF)] * count + chain, "synthesis",
            flops=count * slab // 2, aliases={1: count, 2: count + 1} if chain else {},
        )(f, far_basis, part)
        if chain:
            far_basis, part = outs[count:]
        fields += [send(o, GRP, s) if s else o for s, o in zip(shifts, outs)]
    return call(finish_body, 10, one(pts // 8, C, BF), "finish")(total, linear, *fields)


def solution(mesh):
    fine = Mesh(mesh.devices.reshape([SIZES[a] for a in ALL]), ALL)
    return jax.shard_map(
        on_device,
        mesh=fine,
        in_specs=(
            P(PTS, None),
            P(None, PTS),
            P(PTS),
            P(),
            P(ALL, None, None, None),
            P(),
            P(),
        ),
        out_specs=P(ALL, None),
        check_vma=False,
    )
```

```python
import functools
import math

import jax
import jax.numpy as jnp
from jax import lax
from jax.experimental import pallas as pl
from jax.experimental.pallas import tpu as pltpu
from jax.sharding import Mesh, PartitionSpec as P

SIZES = {"z_hi": 4, "x": 4, "core": 2, "y": 4, "z_lo": 2}
PTS = ("z_hi", "x", "core")
GRP = ("y", "z_lo")
ALL = PTS + GRP
FAR_LAST = (1, 3, 2)
C = 128
PITCH = C + 1
ROWS = 32
BF, F32 = jnp.bfloat16, jnp.float32
VM = pl.BlockSpec(memory_space=pltpu.VMEM)
SM = pl.BlockSpec(memory_space=pltpu.SMEM)


def call(body, n_in, out_shape, name, scratch=(), smem=0, flops=0, aliases={}, last=(), room=16):
    many = isinstance(out_shape, (list, tuple))
    return pl.pallas_call(
        body,
        in_specs=[SM] * smem + [VM] * n_in + [pl.BlockSpec(memory_space=m) for m in last],
        out_specs=[VM] * len(out_shape) if many else VM,
        out_shape=out_shape,
        scratch_shapes=list(scratch),
        compiler_params=pltpu.CompilerParams(vmem_limit_bytes=room * 2**20),
        input_output_aliases=aliases,
        cost_estimate=pl.CostEstimate(flops=flops, bytes_accessed=2**20, transcendentals=0),
        name=name,
    )


def send(value, axes, shift):
    n = 1
    for a in axes:
        n *= SIZES[a]
    return lax.ppermute(value, axes, [(j, (j + shift) % n) for j in range(n)])


def turn(x):
    h = math.pi * (x - jnp.round(x))
    q = h * h
    s = c = None
    for k in range(6, -1, -1):
        a = (-1) ** k / math.factorial(2 * k + 1)
        s = a if s is None else s * q + a
    for k in range(7, -1, -1):
        a = (-1) ** k / math.factorial(2 * k)
        c = a if c is None else c * q + a
    s = s * h
    return 1.0 - 2.0 * s * s, -2.0 * s * c


def times(a, b):
    return a[0] * b[0] - a[1] * b[1], a[0] * b[1] + a[1] * b[0]


def powers(x, n):
    one = turn(x)
    out = [(jnp.ones_like(x), jnp.zeros_like(x)), one]
    for k in range(2, n):
        out.append(times(out[k // 2], out[k - k // 2]))
    return out


def build_tables(coords, exy, ez, sl):
    for k, v in enumerate(powers(coords[2], 32)):
        ez[k, 0, sl], ez[k, 1, sl] = v
    px, py = powers(coords[0], 9), powers(coords[1], 9)
    signed = lambda p, k: p[k] if k >= 0 else (p[-k][0], -p[-k][1])
    for kx in range(-8, 8):
        for ky in range(-8, 8):
            k = (kx + 8) * 16 + ky + 8
            exy[k, 0, sl], exy[k, 1, sl] = times(signed(px, kx), signed(py, ky))


def lanes3(value):
    hi = value.astype(BF).astype(F32)
    mid = (value - hi).astype(BF).astype(F32)
    low = value - hi - mid
    lane = lax.broadcasted_iota(jnp.int32, (16, C), 1)
    return jnp.where(lane == 0, hi, jnp.where(lane == 1, mid, jnp.where(lane == 2, low, 0.0))).astype(BF)


def total_of(rows):
    lane = lax.broadcasted_iota(jnp.int32, (1, C), 1)
    return jnp.sum(jnp.where(lane < 3, rows[:1], 0.0), axis=1, keepdims=True)


def analyse(index, row, put_coef, put_basis, exy, ez, w, scr):
    @pl.loop(0, C // 16)
    def _(it):
        for u in range(16):
            m = it * 16 + u
            k = index[row, m]
            ixy, iz = lax.shift_right_logical(k, 5), lax.bitwise_and(k, 31)
            for j in range(ROWS // 8):
                sl = pl.ds(8 * j, 8)
                re, im = times((exy[ixy, 0, sl], exy[ixy, 1, sl]), (ez[iz, 0, sl], ez[iz, 1, sl]))
                scr[pl.ds(8 * j * PITCH + m, 8, stride=PITCH), :] = re
                scr[pl.ds((ROWS + 8 * j) * PITCH + m, 8, stride=PITCH), :] = im

    acc = None
    for k in range(4):
        cols = pl.ds(k * 1024, 1024)
        both = []
        for part in range(2):
            rows = [scr[pl.ds((part * ROWS + k * 8 + h) * PITCH, C), :].astype(BF) for h in range(8)]
            both.append(jnp.concatenate(rows, axis=1))
        both = jnp.concatenate(both, axis=0)
        put_basis(cols, both)
        term = jnp.dot(both, w[cols, :], preferred_element_type=F32)
        acc = term if acc is None else acc + term
    put_coef(acc.astype(BF))


def slabs(count, first, index, coef, basis, exy, ez, w, quad, scr):
    @pl.loop(0, count)
    def _(s):
        def put_coef(value):
            coef[pl.ds(pl.multiple_of(s * 2 * C, 2 * C), 2 * C), :] = value

        def put_basis(cols, value):
            basis[pl.ds(pl.multiple_of((first % 4 + s) * 2 * C, 2 * C), 2 * C), cols] = value

        analyse(index, first + s, put_coef, put_basis, exy, ez, w, scr)

    total = jnp.sum(jnp.sum(quad[...], axis=0, keepdims=True), axis=1, keepdims=True)
    coef[pl.ds(count * 2 * C, 16), :] = lanes3(total)


def pack_index(table, index):
    z, x, core = (lax.axis_index(a) for a in PTS)
    group = lax.axis_index("y") * 2 + lax.axis_index("z_lo")
    tile, within = group // 4, lax.rem(group, 4)
    part = lax.broadcasted_iota(jnp.int32, (1, C), 1) // 32
    for flip in range(2):
        for dx in range(4):
            row = jnp.zeros((1, C), jnp.int32)
            for dz in range(4):
                own = (lax.rem(z + dz, 4) * 4 + lax.rem(x + dx, 4)) * 2 + lax.rem(core + flip, 2)
                v = table[:, pl.ds(pl.multiple_of(own * 256 + tile * C, C), C)]
                k = ((v[0:1] + 8) * 16 + v[1:2] + 8) * 32 + v[2:3]
                k = pltpu.roll(k, lax.rem(dz - within + 4, 4) * 32, 1)
                row = jnp.where(part == dz, k, row)
            index[pl.ds(flip * 4 + dx, 1), :] = row


def first_body(*refs):
    given, (coef, basis, exy, ez, w, linear, quad, index) = refs[:6], refs[6:14]
    scr, coords, table, lin, bias, f, held, sems = refs[14:]
    here = (coords, table, quad, lin, bias, f)
    loads = [pltpu.make_async_copy(src, dst, sems.at[i]) for i, (src, dst) in enumerate(zip(given, here))]
    for load in loads:
        load.start()
    loads[0].wait()

    @pl.loop(0, ROWS // 8)
    def _(o):
        row = lambda i, r: coords[pl.ds(i, 1), pl.ds(pl.multiple_of((8 * o + r) * C, C), C)]
        at = [jnp.concatenate([row(i, r) for r in range(8)], axis=0) for i in range(3)]
        build_tables(at, exy, ez, pl.ds(pl.multiple_of(8 * o, 8), 8))

    loads[1].wait()
    pack_index(table, index)
    hold = pltpu.make_async_copy(index, held, sems.at[6])
    hold.start()
    for load in loads[2:]:
        load.wait()
    columns = quad[...].T
    for o in range(ROWS):
        rows = pl.ds(o * C, C)
        w[rows, :] = (f[rows, :].astype(F32) * columns[:, o : o + 1]).astype(BF)
    group = lax.axis_index("y") * 2 + lax.axis_index("z_lo")
    mine = f[pl.ds(pl.multiple_of(group * 512, 512), 512), :]
    linear[...] = jnp.dot(mine, lin[...], preferred_element_type=F32) + bias[...]
    hold.wait()
    slabs(4, 4, held, coef, basis, exy, ez, w, quad, scr)


def near_body(count, first, index, quad, exy, ez, w, given, coef, basis, scr):
    slabs(count, first, index, coef, basis, exy, ez, w, quad, scr)


def pair_body(own, got, *outs):
    tail = total_of(own[pl.ds(6 * C, 16), :].astype(F32) + got[pl.ds(8 * C, 16), :].astype(F32))
    for s, out in enumerate(outs):
        summed = own[pl.ds(s * 2 * C, 2 * C), :].astype(F32) + got[pl.ds((s + 1) * 2 * C, 2 * C), :].astype(F32)
        out[pl.ds(0, 2 * C), :] = summed.astype(BF)
        out[pl.ds(2 * C, 16), :] = lanes3(tail)


def x_body(own, got0, got1, got2, got3, keep, out1, out2, out3):
    body, rest = pl.ds(0, 2 * C), pl.ds(2 * C, 16)
    summed = own[body, :].astype(F32) + got0[body, :].astype(F32)
    tail = own[rest, :].astype(F32) + got0[pl.ds(8 * C, 16), :].astype(F32)
    for g in (got1, got2, got3):
        summed = summed + g[body, :].astype(F32)
        tail = tail + g[rest, :].astype(F32)
    tail = lanes3(total_of(tail))
    for part in range(2):
        cols = pl.ds(part * C, C)
        for s, ref in enumerate((keep, out1, out2, out3)):
            at = part * C + s * 32
            ref[pl.ds(0, 32), cols] = summed[at : at + 32].astype(ref.dtype)
            ref[pl.ds(32, 16), cols] = tail.astype(ref.dtype)


def filter_body(own, got1, got2, got3, weight, out, total):
    summed = own[...]
    for g in (got1, got2, got3):
        summed = summed + g[...].astype(F32)
    total[...] = jnp.broadcast_to(total_of(summed[32:, :C]), total.shape)
    row = lax.rem(lax.broadcasted_iota(jnp.int32, (16, 2 * C), 0), 8)
    for g in range(4):
        block = summed[8 * g : 8 * g + 8]
        lhs = jnp.concatenate([block[:, :C], block[:, C:]], axis=0).astype(BF)
        picked = jnp.zeros((16, 2 * C), F32)
        for i in range(8):
            m = 8 * g + i
            both = jnp.concatenate([weight[m, 0], weight[m, 1]], axis=1)
            picked = jnp.where(row == i, jnp.dot(lhs, both, preferred_element_type=F32), picked)
        real = picked[:8, :C] - picked[8:, C:]
        imag = picked[:8, C:] + picked[8:, :C]
        out[pl.ds(8 * g, 8), :] = jnp.concatenate([real, imag], axis=1).astype(BF)


def turned_body(src, out):
    for dx in range(4):
        for part in range(2):
            block = src[pl.ds(dx * C, C), pl.ds(part * C, C)].astype(F32).T
            out[:, pl.ds((dx * 2 + part) * C, C)] = block.astype(BF)


def near_field_body(src, basis, part, f):
    turned_body(src, f)
    for k in range(8):
        at = pl.ds(k * 512, 512)
        part[:, at] = jnp.dot(f[...], basis[:, at], preferred_element_type=F32)


def synthesis_body(flip, steps, f, basis, part, out, *_):
    y, z_lo = lax.axis_index("y"), lax.axis_index("z_lo")
    for i, dy in enumerate(steps):
        owner = lax.rem(y + dy, 4) * 2 + lax.rem(z_lo + flip, 2)
        at = pl.ds(pl.multiple_of(owner * 512, 512), 512)
        value = part[:, at] + jnp.dot(f[...], basis[:, at], preferred_element_type=F32)
        out[pl.ds(i * C, C), :] = value.astype(out.dtype)


def merge_body(own, got, *outs):
    for i, out in enumerate(outs):
        rows = pl.ds(i * C, C)
        out[...] = (own[rows, :] + got[rows, :].astype(F32)).astype(BF)


def finish_body(total, linear, own, got, *rest):
    *blocks, out = rest
    summed = own[pl.ds(3 * C, C), :] + got[...].astype(F32)
    for b in blocks:
        summed = summed + b[...].astype(F32)
    scaled = summed / total[0:1, 0:1]
    for k in range(4):
        rows = pl.ds(k * C, C)
        pre = scaled[:, k * C : k * C + C].T + linear[rows, :]
        out[rows, :] = (0.5 * pre * (1.0 + lax.erf(pre * math.sqrt(0.5)))).astype(BF)


def join_body(piece, *rest):
    *got, out = rest
    rows = piece.shape[0]
    for s, ref in zip((0, *FAR_LAST), (piece, *got)):
        out[pl.ds(s * rows, rows), :] = ref[...]


def gather_over(piece, axes, n):
    got = [send(piece, axes, n - s) for s in FAR_LAST]
    shape = jax.ShapeDtypeStruct((n * piece.shape[0], piece.shape[1]), piece.dtype)
    return call(join_body, n, shape, "join")(piece, *got)


def on_device(features, coords, quad_weight, mode_table, mode_weight, lin_weight, bias):
    pts = features.shape[0]
    scr = pltpu.VMEM((2 * ROWS * PITCH, C), F32)
    one = lambda rows, cols, dt: jax.ShapeDtypeStruct((rows, cols), dt)
    slab = 2 * 2 * C * pts * C
    far, far_basis, exy, ez, w, linear, quad, index = call(
        first_body, 0,
        [pltpu.VMEM((8 * C + 16, C), BF), pltpu.VMEM((8 * C, pts), BF), pltpu.VMEM((256, 2, ROWS, C), F32),
         pltpu.VMEM((32, 2, ROWS, C), F32), pltpu.VMEM((pts, C), BF), pltpu.VMEM((pts // 8, C), F32),
         pltpu.VMEM((ROWS, C), F32), pltpu.VMEM((8, C), jnp.int32)],
        "first",
        [scr, pltpu.VMEM((3, pts), F32), pltpu.VMEM((3, 8192), jnp.int32), pltpu.VMEM((C, C), BF), pltpu.VMEM((1, C), F32),
         pltpu.VMEM((pts, C), BF), pltpu.SMEM((8, C), jnp.int32), pltpu.SemaphoreType.DMA((7,))],
        0, 8 * slab, last=[pltpu.HBM] * 6, room=42,
    )(coords, mode_table, quad_weight.reshape(ROWS, C), lin_weight, bias.reshape(1, C), features)
    got = send(far, ("core",), 1)

    def near(count, first, given, alias):
        return call(
            functools.partial(near_body, count, first), 4,
            [pltpu.VMEM((count * 2 * C + 16, C), BF), pltpu.VMEM((8 * C, pts), BF)],
            "near", [scr], 1, 2 * count * slab, last=[pltpu.VMEM if alias else pl.ANY], aliases={5: 1} if alias else {},
        )(index, quad, exy, ez, w, given)

    mine, basis = near(3, 1, linear, False)
    outs = call(pair_body, 2, [one(2 * C + 16, C, BF)] * 3, "pair")(mine, got)
    across = {s: send(outs[s - 1], ("x",), s) for s in FAR_LAST}
    mine, basis = near(1, 0, basis, True)
    keep, *outs = call(x_body, 5, [one(48, 2 * C, F32)] + [one(48, 2 * C, BF)] * 3, "x_sum")(
        mine, got, *[across[s] for s in FAR_LAST]
    )
    got = [send(outs[s - 1], ("z_hi",), s) for s in FAR_LAST]
    piece, total = call(filter_body, 5, [one(32, 2 * C, BF), one(8, C, F32)], "filter")(keep, *got, mode_weight)
    piece = gather_over(piece, ("z_hi",), 4)
    piece = gather_over(piece, ("x",), 4)
    other = send(piece, ("core",), 1)
    part = call(
        near_field_body, 2, pltpu.VMEM((C, pts), F32), "near_field", [pltpu.VMEM((C, 8 * C), BF)], flops=4 * slab
    )(piece, basis)
    f = call(turned_body, 1, one(C, 8 * C, BF), "turned")(other)
    steps = (*FAR_LAST, 0)

    def field(flip, steps, dtype, basis, part, last=False):
        chain = [] if last else [pltpu.VMEM(v.shape, v.dtype) for v in (basis, part)]
        return call(
            functools.partial(synthesis_body, flip, steps), 3, [one(len(steps) * C, 512, dtype)] + chain, "synthesis",
            flops=len(steps) * slab // 2, aliases={1: 1, 2: 2} if chain else {},
        )(f, basis, part)

    out, far_basis, part = field(1, steps[:3], BF, far_basis, part)
    got0 = send(out, ("z_lo",), 1)
    out, far_basis, part = field(1, steps[3:], BF, far_basis, part)
    got1 = send(out, ("z_lo",), 1)
    (own,) = field(0, steps, F32, far_basis, part, True)
    outs = call(merge_body, 2, [one(C, 512, BF)] * 3, "merge")(own, got0)
    fields = [send(o, ("y",), s) for o, s in zip(outs, steps)]
    return call(finish_body, 7, one(pts // 8, C, BF), "finish")(total, linear, own, got1, *fields)


def solution(mesh):
    fine = Mesh(mesh.devices.reshape([SIZES[a] for a in ALL]), ALL)
    return jax.shard_map(
        on_device,
        mesh=fine,
        in_specs=(
            P(PTS, None),
            P(None, PTS),
            P(PTS),
            P(),
            P(ALL, None, None, None),
            P(),
            P(),
        ),
        out_specs=P(ALL, None),
        check_vma=False,
    )
```

```python
import functools
import math

import jax
import jax.numpy as jnp
from jax import lax
from jax.experimental import pallas as pl
from jax.experimental.pallas import tpu as pltpu
from jax.sharding import Mesh, PartitionSpec as P

SIZES = {"z_hi": 4, "x": 4, "core": 2, "y": 4, "z_lo": 2}
PTS = ("z_hi", "x", "core")
GRP = ("y", "z_lo")
ALL = PTS + GRP
FAR_LAST = (1, 3, 2)
C = 128
PITCH = C + 1
ROWS = 32
BF, F32 = jnp.bfloat16, jnp.float32
VM = pl.BlockSpec(memory_space=pltpu.VMEM)
SM = pl.BlockSpec(memory_space=pltpu.SMEM)


def call(body, n_in, out_shape, name, scratch=(), smem=0, flops=0, aliases={}, last=(), room=16):
    many = isinstance(out_shape, (list, tuple))
    return pl.pallas_call(
        body,
        in_specs=[SM] * smem + [VM] * n_in + [pl.BlockSpec(memory_space=m) for m in last],
        out_specs=[VM] * len(out_shape) if many else VM,
        out_shape=out_shape,
        scratch_shapes=list(scratch),
        compiler_params=pltpu.CompilerParams(vmem_limit_bytes=room * 2**20),
        input_output_aliases=aliases,
        cost_estimate=pl.CostEstimate(flops=flops, bytes_accessed=2**20, transcendentals=0),
        name=name,
    )


def send(value, axes, shift):
    n = 1
    for a in axes:
        n *= SIZES[a]
    return lax.ppermute(value, axes, [(j, (j + shift) % n) for j in range(n)])


def turn(x):
    h = math.pi * (x - jnp.round(x))
    q = h * h
    s = c = None
    for k in range(6, -1, -1):
        a = (-1) ** k / math.factorial(2 * k + 1)
        s = a if s is None else s * q + a
    for k in range(7, -1, -1):
        a = (-1) ** k / math.factorial(2 * k)
        c = a if c is None else c * q + a
    s = s * h
    return 1.0 - 2.0 * s * s, -2.0 * s * c


def times(a, b):
    return a[0] * b[0] - a[1] * b[1], a[0] * b[1] + a[1] * b[0]


def powers(x, n):
    one = turn(x)
    out = [(jnp.ones_like(x), jnp.zeros_like(x)), one]
    for k in range(2, n):
        out.append(times(out[k // 2], out[k - k // 2]))
    return out


def build_tables(coords, exy, ez, sl):
    for k, v in enumerate(powers(coords[2], 32)):
        ez[k, 0, sl], ez[k, 1, sl] = v
    px, py = powers(coords[0], 9), powers(coords[1], 9)
    signed = lambda p, k: p[k] if k >= 0 else (p[-k][0], -p[-k][1])
    for kx in range(-8, 8):
        for ky in range(-8, 8):
            k = (kx + 8) * 16 + ky + 8
            exy[k, 0, sl], exy[k, 1, sl] = times(signed(px, kx), signed(py, ky))


def lanes3(value):
    hi = value.astype(BF).astype(F32)
    mid = (value - hi).astype(BF).astype(F32)
    low = value - hi - mid
    lane = lax.broadcasted_iota(jnp.int32, (16, C), 1)
    return jnp.where(lane == 0, hi, jnp.where(lane == 1, mid, jnp.where(lane == 2, low, 0.0))).astype(BF)


def total_of(rows):
    lane = lax.broadcasted_iota(jnp.int32, (1, C), 1)
    return jnp.sum(jnp.where(lane < 3, rows[:1], 0.0), axis=1, keepdims=True)


def analyse(index, row, put_coef, put_basis, exy, ez, w, scr):
    @pl.loop(0, C // 16)
    def _(it):
        for u in range(16):
            m = it * 16 + u
            k = index[row, m]
            ixy, iz = lax.shift_right_logical(k, 5), lax.bitwise_and(k, 31)
            for j in range(ROWS // 8):
                sl = pl.ds(8 * j, 8)
                re, im = times((exy[ixy, 0, sl], exy[ixy, 1, sl]), (ez[iz, 0, sl], ez[iz, 1, sl]))
                scr[pl.ds(8 * j * PITCH + m, 8, stride=PITCH), :] = re
                scr[pl.ds((ROWS + 8 * j) * PITCH + m, 8, stride=PITCH), :] = im

    acc = None
    for k in range(4):
        cols = pl.ds(k * 1024, 1024)
        both = []
        for part in range(2):
            rows = [scr[pl.ds((part * ROWS + k * 8 + h) * PITCH, C), :].astype(BF) for h in range(8)]
            both.append(jnp.concatenate(rows, axis=1))
        both = jnp.concatenate(both, axis=0)
        put_basis(cols, both)
        term = jnp.dot(both, w[cols, :], preferred_element_type=F32)
        acc = term if acc is None else acc + term
    put_coef(acc.astype(BF))


def slabs(count, first, index, coef, basis, exy, ez, w, quad, scr):
    @pl.loop(0, count)
    def _(s):
        def put_coef(value):
            coef[pl.ds(pl.multiple_of(s * 2 * C, 2 * C), 2 * C), :] = value

        def put_basis(cols, value):
            basis[pl.ds(pl.multiple_of((first % 4 + s) * 2 * C, 2 * C), 2 * C), cols] = value

        analyse(index, first + s, put_coef, put_basis, exy, ez, w, scr)

    total = jnp.sum(jnp.sum(quad[...], axis=0, keepdims=True), axis=1, keepdims=True)
    coef[pl.ds(count * 2 * C, 16), :] = lanes3(total)


def pack_index(table, index):
    z, x, core = (lax.axis_index(a) for a in PTS)
    group = lax.axis_index("y") * 2 + lax.axis_index("z_lo")
    tile, within = group // 4, lax.rem(group, 4)
    part = lax.broadcasted_iota(jnp.int32, (1, C), 1) // 32
    for flip in range(2):
        for dx in range(4):
            row = jnp.zeros((1, C), jnp.int32)
            for dz in range(4):
                own = (lax.rem(z + dz, 4) * 4 + lax.rem(x + dx, 4)) * 2 + lax.rem(core + flip, 2)
                v = table[:, pl.ds(pl.multiple_of(own * 256 + tile * C, C), C)]
                k = ((v[0:1] + 8) * 16 + v[1:2] + 8) * 32 + v[2:3]
                k = pltpu.roll(k, lax.rem(dz - within + 4, 4) * 32, 1)
                row = jnp.where(part == dz, k, row)
            index[pl.ds(flip * 4 + dx, 1), :] = row


def first_body(*refs):
    given, (coef, basis, exy, ez, w, linear, quad, index) = refs[:6], refs[6:14]
    scr, coords, table, lin, bias, f, held, sems = refs[14:]
    here = (coords, table, quad, lin, bias, f)
    loads = [pltpu.make_async_copy(src, dst, sems.at[i]) for i, (src, dst) in enumerate(zip(given, here))]
    for load in loads:
        load.start()
    loads[0].wait()

    @pl.loop(0, ROWS // 8)
    def _(o):
        row = lambda i, r: coords[pl.ds(i, 1), pl.ds(pl.multiple_of((8 * o + r) * C, C), C)]
        at = [jnp.concatenate([row(i, r) for r in range(8)], axis=0) for i in range(3)]
        build_tables(at, exy, ez, pl.ds(pl.multiple_of(8 * o, 8), 8))

    loads[1].wait()
    pack_index(table, index)
    hold = pltpu.make_async_copy(index, held, sems.at[6])
    hold.start()
    for load in loads[2:]:
        load.wait()
    columns = quad[...].T
    for o in range(ROWS):
        rows = pl.ds(o * C, C)
        w[rows, :] = (f[rows, :].astype(F32) * columns[:, o : o + 1]).astype(BF)
    group = lax.axis_index("y") * 2 + lax.axis_index("z_lo")
    mine = f[pl.ds(pl.multiple_of(group * 512, 512), 512), :]
    linear[...] = jnp.dot(mine, lin[...], preferred_element_type=F32) + bias[...]
    hold.wait()
    slabs(4, 4, held, coef, basis, exy, ez, w, quad, scr)


def near_body(count, first, index, quad, exy, ez, w, given, coef, basis, scr):
    slabs(count, first, index, coef, basis, exy, ez, w, quad, scr)


def pair_body(own, got, *outs):
    tail = total_of(own[pl.ds(6 * C, 16), :].astype(F32) + got[pl.ds(8 * C, 16), :].astype(F32))
    for s, out in enumerate(outs):
        summed = own[pl.ds(s * 2 * C, 2 * C), :].astype(F32) + got[pl.ds((s + 1) * 2 * C, 2 * C), :].astype(F32)
        out[pl.ds(0, 2 * C), :] = summed.astype(BF)
        out[pl.ds(2 * C, 16), :] = lanes3(tail)


def x_body(own, got0, got1, got2, got3, keep, out1, out2, out3):
    body, rest = pl.ds(0, 2 * C), pl.ds(2 * C, 16)
    summed = own[body, :].astype(F32) + got0[body, :].astype(F32)
    tail = own[rest, :].astype(F32) + got0[pl.ds(8 * C, 16), :].astype(F32)
    for g in (got1, got2, got3):
        summed = summed + g[body, :].astype(F32)
        tail = tail + g[rest, :].astype(F32)
    tail = lanes3(total_of(tail))
    for part in range(2):
        cols = pl.ds(part * C, C)
        for s, ref in enumerate((keep, out1, out2, out3)):
            at = part * C + s * 32
            ref[pl.ds(0, 32), cols] = summed[at : at + 32].astype(ref.dtype)
            ref[pl.ds(32, 16), cols] = tail.astype(ref.dtype)


def filter_body(own, got1, got2, got3, weight, out, total):
    summed = own[...]
    for g in (got1, got2, got3):
        summed = summed + g[...].astype(F32)
    total[...] = jnp.broadcast_to(total_of(summed[32:, :C]), total.shape)
    row = lax.rem(lax.broadcasted_iota(jnp.int32, (16, 2 * C), 0), 8)
    for g in range(4):
        block = summed[8 * g : 8 * g + 8]
        lhs = jnp.concatenate([block[:, :C], block[:, C:]], axis=0).astype(BF)
        picked = jnp.zeros((16, 2 * C), F32)
        for i in range(8):
            m = 8 * g + i
            both = jnp.concatenate([weight[m, 0], weight[m, 1]], axis=1)
            picked = jnp.where(row == i, jnp.dot(lhs, both, preferred_element_type=F32), picked)
        real = picked[:8, :C] - picked[8:, C:]
        imag = picked[:8, C:] + picked[8:, :C]
        out[pl.ds(8 * g, 8), :] = jnp.concatenate([real, imag], axis=1).astype(BF)


def turned_body(src, out):
    for dx in range(4):
        for part in range(2):
            block = src[pl.ds(dx * C, C), pl.ds(part * C, C)].astype(F32).T
            out[:, pl.ds((dx * 2 + part) * C, C)] = block.astype(BF)


def near_field_body(src, basis, part, f):
    turned_body(src, f)
    for k in range(8):
        at = pl.ds(k * 512, 512)
        part[:, at] = jnp.dot(f[...], basis[:, at], preferred_element_type=F32)


def synthesis_body(places, f, basis, part, out, *_):
    y, z_lo = lax.axis_index("y"), lax.axis_index("z_lo")
    for i, (flip, dy) in enumerate(places):
        owner = lax.rem(y + dy, 4) * 2 + lax.rem(z_lo + flip, 2)
        at = pl.ds(pl.multiple_of(owner * 512, 512), 512)
        value = part[:, at] + jnp.dot(f[...], basis[:, at], preferred_element_type=F32)
        out[pl.ds(i * C, C), :] = value.astype(out.dtype)


def merge_body(pairs, own, got, *outs):
    for (mine, theirs), out in zip(pairs, outs, strict=True):
        out[...] = (own[pl.ds(mine * C, C), :] + got[pl.ds(theirs * C, C), :].astype(F32)).astype(BF)


def finish_body(total, linear, own, *rest):
    *blocks, out = rest
    summed = own[pl.ds(3 * C, C), :]
    for b in blocks:
        summed = summed + b[pl.ds(0, C), :].astype(F32)
    scaled = summed / total[0:1, 0:1]
    for k in range(4):
        rows = pl.ds(k * C, C)
        pre = scaled[:, k * C : k * C + C].T + linear[rows, :]
        out[rows, :] = (0.5 * pre * (1.0 + lax.erf(pre * math.sqrt(0.5)))).astype(BF)


def join_body(piece, *rest):
    *got, out = rest
    rows = piece.shape[0]
    for s, ref in zip((0, 2, 3, 1), (piece, *got)):
        out[pl.ds(s * rows, rows), :] = ref[...]


def gather_over(piece, axes, n):
    got = [send(piece, axes, n - s) for s in (2, 3, 1)]
    shape = jax.ShapeDtypeStruct((n * piece.shape[0], piece.shape[1]), piece.dtype)
    return call(join_body, n, shape, "join")(piece, *got)


def on_device(features, coords, quad_weight, mode_table, mode_weight, lin_weight, bias):
    pts = features.shape[0]
    scr = pltpu.VMEM((2 * ROWS * PITCH, C), F32)
    one = lambda rows, cols, dt: jax.ShapeDtypeStruct((rows, cols), dt)
    slab = 2 * 2 * C * pts * C
    far, far_basis, exy, ez, w, linear, quad, index = call(
        first_body, 0,
        [pltpu.VMEM((8 * C + 16, C), BF), pltpu.VMEM((8 * C, pts), BF), pltpu.VMEM((256, 2, ROWS, C), F32),
         pltpu.VMEM((32, 2, ROWS, C), F32), pltpu.VMEM((pts, C), BF), pltpu.VMEM((pts // 8, C), F32),
         pltpu.VMEM((ROWS, C), F32), pltpu.VMEM((8, C), jnp.int32)],
        "first",
        [scr, pltpu.VMEM((3, pts), F32), pltpu.VMEM((3, 8192), jnp.int32), pltpu.VMEM((C, C), BF), pltpu.VMEM((1, C), F32),
         pltpu.VMEM((pts, C), BF), pltpu.SMEM((8, C), jnp.int32), pltpu.SemaphoreType.DMA((7,))],
        0, 8 * slab, last=[pltpu.HBM] * 6, room=42,
    )(coords, mode_table, quad_weight.reshape(ROWS, C), lin_weight, bias.reshape(1, C), features)
    got = send(far, ("core",), 1)

    def near(count, first, given, alias):
        return call(
            functools.partial(near_body, count, first), 4,
            [pltpu.VMEM((count * 2 * C + 16, C), BF), pltpu.VMEM((8 * C, pts), BF)],
            "near", [scr], 1, 2 * count * slab, last=[pltpu.VMEM if alias else pl.ANY], aliases={5: 1} if alias else {},
        )(index, quad, exy, ez, w, given)

    mine, basis = near(3, 1, linear, False)
    outs = call(pair_body, 2, [one(2 * C + 16, C, BF)] * 3, "pair")(mine, got)
    across = {s: send(outs[s - 1], ("x",), s) for s in FAR_LAST}
    mine, basis = near(1, 0, basis, True)
    keep, *outs = call(x_body, 5, [one(48, 2 * C, F32)] + [one(48, 2 * C, BF)] * 3, "x_sum")(
        mine, got, *[across[s] for s in FAR_LAST]
    )
    got = [send(outs[s - 1], ("z_hi",), s) for s in FAR_LAST]
    piece, total = call(filter_body, 5, [one(32, 2 * C, BF), one(8, C, F32)], "filter")(keep, *got, mode_weight)
    piece = gather_over(piece, ("z_hi",), 4)
    piece = gather_over(piece, ("x",), 4)
    other = send(piece, ("core",), 1)
    part = call(
        near_field_body, 2, pltpu.VMEM((C, pts), F32), "near_field", [pltpu.VMEM((C, 8 * C), BF)], flops=4 * slab
    )(piece, basis)
    f = call(turned_body, 1, one(C, 8 * C, BF), "turned")(other)
    def field(places, dtype, basis, part, last=False):
        chain = [] if last else [pltpu.VMEM(v.shape, v.dtype) for v in (basis, part)]
        return call(
            functools.partial(synthesis_body, places), 3, [one(len(places) * C, 512, dtype)] + chain, "synthesis",
            flops=len(places) * slab // 2, aliases={1: 1, 2: 2} if chain else {},
        )(f, basis, part)

    def merge(*pairs):
        return call(functools.partial(merge_body, pairs), 2, [one(C, 512, BF)] * len(pairs), "merge")

    out, far_basis, part = field(((1, 1), (1, 3)), BF, far_basis, part)
    beside = send(out, ("z_lo",), 1)
    out, far_basis, part = field(((0, 2), (1, 2)), BF, far_basis, part)
    across = send(out, ("y",), 2)
    (own,) = field(((0, 1), (0, 3), (1, 0), (0, 0)), F32, far_basis, part, True)
    one_step, three_steps = merge((0, 0), (1, 1))(own, beside)
    (out,) = merge((2, 1))(own, across)
    fields = [across, send(one_step, ("y",), 1), send(three_steps, ("y",), 3), send(out, ("z_lo",), 1)]
    return call(finish_body, 7, one(pts // 8, C, BF), "finish")(total, linear, own, *fields)


def solution(mesh):
    fine = Mesh(mesh.devices.reshape([SIZES[a] for a in ALL]), ALL)
    return jax.shard_map(
        on_device,
        mesh=fine,
        in_specs=(
            P(PTS, None),
            P(None, PTS),
            P(PTS),
            P(),
            P(ALL, None, None, None),
            P(),
            P(),
        ),
        out_specs=P(ALL, None),
        check_vma=False,
    )
```

```python
import functools
import math

import jax
import jax.numpy as jnp
from jax import lax
from jax.experimental import pallas as pl
from jax.experimental.pallas import tpu as pltpu
from jax.sharding import Mesh, PartitionSpec as P

SIZES = {"z_hi": 4, "x": 4, "core": 2, "y": 4, "z_lo": 2}
PTS = ("z_hi", "x", "core")
GRP = ("y", "z_lo")
ALL = PTS + GRP
FAR_LAST = (1, 3, 2)
C = 128
PITCH = C + 1
ROWS = 32
BF, F32 = jnp.bfloat16, jnp.float32
VM = pl.BlockSpec(memory_space=pltpu.VMEM)
SM = pl.BlockSpec(memory_space=pltpu.SMEM)


def call(body, n_in, out_shape, name, scratch=(), smem=0, flops=0, aliases={}, last=(), room=16):
    many = isinstance(out_shape, (list, tuple))
    return pl.pallas_call(
        body,
        in_specs=[SM] * smem + [VM] * n_in + [pl.BlockSpec(memory_space=m) for m in last],
        out_specs=[VM] * len(out_shape) if many else VM,
        out_shape=out_shape,
        scratch_shapes=list(scratch),
        compiler_params=pltpu.CompilerParams(vmem_limit_bytes=room * 2**20),
        input_output_aliases=aliases,
        cost_estimate=pl.CostEstimate(flops=flops, bytes_accessed=2**20, transcendentals=0),
        name=name,
    )


def send(value, axes, shift):
    n = 1
    for a in axes:
        n *= SIZES[a]
    return lax.ppermute(value, axes, [(j, (j + shift) % n) for j in range(n)])


def turn(x):
    h = math.pi * (x - jnp.round(x))
    q = h * h
    s = c = None
    for k in range(6, -1, -1):
        a = (-1) ** k / math.factorial(2 * k + 1)
        s = a if s is None else s * q + a
    for k in range(7, -1, -1):
        a = (-1) ** k / math.factorial(2 * k)
        c = a if c is None else c * q + a
    s = s * h
    return 1.0 - 2.0 * s * s, -2.0 * s * c


def times(a, b):
    return a[0] * b[0] - a[1] * b[1], a[0] * b[1] + a[1] * b[0]


def powers(x, n):
    one = turn(x)
    out = [(jnp.ones_like(x), jnp.zeros_like(x)), one]
    for k in range(2, n):
        out.append(times(out[k // 2], out[k - k // 2]))
    return out


def build_tables(coords, exy, ez, sl):
    for k, v in enumerate(powers(coords[2], 32)):
        ez[k, 0, sl], ez[k, 1, sl] = v
    px, py = powers(coords[0], 9), powers(coords[1], 9)
    signed = lambda p, k: p[k] if k >= 0 else (p[-k][0], -p[-k][1])
    for kx in range(-8, 8):
        for ky in range(-8, 8):
            k = (kx + 8) * 16 + ky + 8
            exy[k, 0, sl], exy[k, 1, sl] = times(signed(px, kx), signed(py, ky))


def lanes3(value):
    hi = value.astype(BF).astype(F32)
    mid = (value - hi).astype(BF).astype(F32)
    low = value - hi - mid
    lane = lax.broadcasted_iota(jnp.int32, (16, C), 1)
    return jnp.where(lane == 0, hi, jnp.where(lane == 1, mid, jnp.where(lane == 2, low, 0.0))).astype(BF)


def total_of(rows):
    lane = lax.broadcasted_iota(jnp.int32, (1, C), 1)
    return jnp.sum(jnp.where(lane < 3, rows[:1], 0.0), axis=1, keepdims=True)


def analyse(index, row, put_coef, put_basis, exy, ez, w, scr):
    @pl.loop(0, C // 16)
    def _(it):
        for u in range(16):
            m = it * 16 + u
            k = index[row, m]
            ixy, iz = lax.shift_right_logical(k, 5), lax.bitwise_and(k, 31)
            for j in range(ROWS // 8):
                sl = pl.ds(8 * j, 8)
                re, im = times((exy[ixy, 0, sl], exy[ixy, 1, sl]), (ez[iz, 0, sl], ez[iz, 1, sl]))
                scr[pl.ds(8 * j * PITCH + m, 8, stride=PITCH), :] = re
                scr[pl.ds((ROWS + 8 * j) * PITCH + m, 8, stride=PITCH), :] = im

    acc = None
    for k in range(4):
        cols = pl.ds(k * 1024, 1024)
        both = []
        for part in range(2):
            rows = [scr[pl.ds((part * ROWS + k * 8 + h) * PITCH, C), :].astype(BF) for h in range(8)]
            both.append(jnp.concatenate(rows, axis=1))
        both = jnp.concatenate(both, axis=0)
        put_basis(cols, both)
        term = jnp.dot(both, w[cols, :], preferred_element_type=F32)
        acc = term if acc is None else acc + term
    put_coef(acc.astype(BF))


def slabs(count, first, index, coef, basis, exy, ez, w, quad, scr):
    @pl.loop(0, count)
    def _(s):
        def put_coef(value):
            coef[pl.ds(pl.multiple_of(s * 2 * C, 2 * C), 2 * C), :] = value

        def put_basis(cols, value):
            basis[pl.ds(pl.multiple_of((first % 4 + s) * 2 * C, 2 * C), 2 * C), cols] = value

        analyse(index, first + s, put_coef, put_basis, exy, ez, w, scr)

    total = jnp.sum(jnp.sum(quad[...], axis=0, keepdims=True), axis=1, keepdims=True)
    coef[pl.ds(count * 2 * C, 16), :] = lanes3(total)


def pack_index(table, index):
    z, x, core = (lax.axis_index(a) for a in PTS)
    group = lax.axis_index("y") * 2 + lax.axis_index("z_lo")
    tile, within = group // 4, lax.rem(group, 4)
    part = lax.broadcasted_iota(jnp.int32, (1, C), 1) // 32
    for flip in range(2):
        for dx in range(4):
            row = jnp.zeros((1, C), jnp.int32)
            for dz in range(4):
                own = (lax.rem(z + dz, 4) * 4 + lax.rem(x + dx, 4)) * 2 + lax.rem(core + flip, 2)
                v = table[:, pl.ds(pl.multiple_of(own * 256 + tile * C, C), C)]
                k = ((v[0:1] + 8) * 16 + v[1:2] + 8) * 32 + v[2:3]
                k = pltpu.roll(k, lax.rem(dz - within + 4, 4) * 32, 1)
                row = jnp.where(part == dz, k, row)
            index[pl.ds(flip * 4 + dx, 1), :] = row


def first_body(*refs):
    given, (coef, basis, exy, ez, w, linear, quad, index) = refs[:6], refs[6:14]
    scr, coords, table, lin, bias, f, held, sems = refs[14:]
    here = (coords, table, quad, lin, bias, f)
    loads = [pltpu.make_async_copy(src, dst, sems.at[i]) for i, (src, dst) in enumerate(zip(given, here))]
    for load in loads:
        load.start()
    loads[0].wait()

    @pl.loop(0, ROWS // 8)
    def _(o):
        row = lambda i, r: coords[pl.ds(i, 1), pl.ds(pl.multiple_of((8 * o + r) * C, C), C)]
        at = [jnp.concatenate([row(i, r) for r in range(8)], axis=0) for i in range(3)]
        build_tables(at, exy, ez, pl.ds(pl.multiple_of(8 * o, 8), 8))

    loads[1].wait()
    pack_index(table, index)
    hold = pltpu.make_async_copy(index, held, sems.at[6])
    hold.start()
    for load in loads[2:]:
        load.wait()
    columns = quad[...].T
    for o in range(ROWS):
        rows = pl.ds(o * C, C)
        w[rows, :] = (f[rows, :].astype(F32) * columns[:, o : o + 1]).astype(BF)
    group = lax.axis_index("y") * 2 + lax.axis_index("z_lo")
    mine = f[pl.ds(pl.multiple_of(group * 512, 512), 512), :]
    linear[...] = jnp.dot(mine, lin[...], preferred_element_type=F32) + bias[...]
    hold.wait()
    slabs(4, 4, held, coef, basis, exy, ez, w, quad, scr)


def near_body(count, first, index, quad, exy, ez, w, given, coef, basis, scr):
    slabs(count, first, index, coef, basis, exy, ez, w, quad, scr)


def pair_body(own, got, *outs):
    tail = total_of(own[pl.ds(6 * C, 16), :].astype(F32) + got[pl.ds(8 * C, 16), :].astype(F32))
    for s, out in enumerate(outs):
        summed = own[pl.ds(s * 2 * C, 2 * C), :].astype(F32) + got[pl.ds((s + 1) * 2 * C, 2 * C), :].astype(F32)
        out[pl.ds(0, 2 * C), :] = summed.astype(BF)
        out[pl.ds(2 * C, 16), :] = lanes3(tail)


def x_body(own, got0, got1, got2, got3, keep, out1, out2, out3):
    body, rest = pl.ds(0, 2 * C), pl.ds(2 * C, 16)
    summed = own[body, :].astype(F32) + got0[body, :].astype(F32)
    tail = own[rest, :].astype(F32) + got0[pl.ds(8 * C, 16), :].astype(F32)
    for g in (got1, got2, got3):
        summed = summed + g[body, :].astype(F32)
        tail = tail + g[rest, :].astype(F32)
    tail = lanes3(total_of(tail))
    for part in range(2):
        cols = pl.ds(part * C, C)
        for s, ref in enumerate((keep, out1, out2, out3)):
            at = part * C + s * 32
            ref[pl.ds(0, 32), cols] = summed[at : at + 32].astype(ref.dtype)
            ref[pl.ds(32, 16), cols] = tail.astype(ref.dtype)


def filter_body(own, got1, got2, got3, weight, out, total):
    summed = own[...]
    for g in (got1, got2, got3):
        summed = summed + g[...].astype(F32)
    total[...] = jnp.broadcast_to(total_of(summed[32:, :C]), total.shape)
    row = lax.rem(lax.broadcasted_iota(jnp.int32, (16, 2 * C), 0), 8)
    for g in range(4):
        block = summed[8 * g : 8 * g + 8]
        lhs = jnp.concatenate([block[:, :C], block[:, C:]], axis=0).astype(BF)
        picked = jnp.zeros((16, 2 * C), F32)
        for i in range(8):
            m = 8 * g + i
            both = jnp.concatenate([weight[m, 0], weight[m, 1]], axis=1)
            picked = jnp.where(row == i, jnp.dot(lhs, both, preferred_element_type=F32), picked)
        real = picked[:8, :C] - picked[8:, C:]
        imag = picked[:8, C:] + picked[8:, :C]
        out[pl.ds(8 * g, 8), :] = jnp.concatenate([real, imag], axis=1).astype(BF)


def turned_body(src, out):
    for dx in range(4):
        for part in range(2):
            block = src[pl.ds(dx * C, C), pl.ds(part * C, C)].astype(F32).T
            out[:, pl.ds((dx * 2 + part) * C, C)] = block.astype(BF)


def near_field_body(src, basis, part, f):
    turned_body(src, f)
    for k in range(8):
        at = pl.ds(k * 512, 512)
        part[:, at] = jnp.dot(f[...], basis[:, at], preferred_element_type=F32)


def synthesis_body(places, f, basis, part, out, *_):
    y, z_lo = lax.axis_index("y"), lax.axis_index("z_lo")
    for i, (flip, dy) in enumerate(places):
        owner = lax.rem(y + dy, 4) * 2 + lax.rem(z_lo + flip, 2)
        at = pl.ds(pl.multiple_of(owner * 512, 512), 512)
        value = part[:, at] + jnp.dot(f[...], basis[:, at], preferred_element_type=F32)
        out[pl.ds(i * C, C), :] = value.astype(out.dtype)


def merge_body(pairs, own, got, *outs):
    for (mine, theirs), out in zip(pairs, outs, strict=True):
        out[...] = (own[pl.ds(mine * C, C), :] + got[pl.ds(theirs * C, C), :].astype(F32)).astype(BF)


def finish_body(total, linear, own, *rest):
    *blocks, out = rest
    summed = own[pl.ds(3 * C, C), :]
    for b in blocks:
        summed = summed + b[pl.ds(0, C), :].astype(F32)
    scaled = summed / total[0:1, 0:1]
    for k in range(4):
        rows = pl.ds(k * C, C)
        pre = scaled[:, k * C : k * C + C].T + linear[rows, :]
        out[rows, :] = (0.5 * pre * (1.0 + lax.erf(pre * math.sqrt(0.5)))).astype(BF)


def join_body(piece, *rest):
    *got, out = rest
    rows = piece.shape[0]
    for s, ref in zip((0, *FAR_LAST), (piece, *got)):
        out[pl.ds(s * rows, rows), :] = ref[...]


def gather_over(piece, axes, n):
    got = [send(piece, axes, n - s) for s in FAR_LAST]
    shape = jax.ShapeDtypeStruct((n * piece.shape[0], piece.shape[1]), piece.dtype)
    return call(join_body, n, shape, "join")(piece, *got)


def on_device(features, coords, quad_weight, mode_table, mode_weight, lin_weight, bias):
    pts = features.shape[0]
    scr = pltpu.VMEM((2 * ROWS * PITCH, C), F32)
    one = lambda rows, cols, dt: jax.ShapeDtypeStruct((rows, cols), dt)
    slab = 2 * 2 * C * pts * C
    far, far_basis, exy, ez, w, linear, quad, index = call(
        first_body, 0,
        [pltpu.VMEM((8 * C + 16, C), BF), pltpu.VMEM((8 * C, pts), BF), pltpu.VMEM((256, 2, ROWS, C), F32),
         pltpu.VMEM((32, 2, ROWS, C), F32), pltpu.VMEM((pts, C), BF), pltpu.VMEM((pts // 8, C), F32),
         pltpu.VMEM((ROWS, C), F32), pltpu.VMEM((8, C), jnp.int32)],
        "first",
        [scr, pltpu.VMEM((3, pts), F32), pltpu.VMEM((3, 8192), jnp.int32), pltpu.VMEM((C, C), BF), pltpu.VMEM((1, C), F32),
         pltpu.VMEM((pts, C), BF), pltpu.SMEM((8, C), jnp.int32), pltpu.SemaphoreType.DMA((7,))],
        0, 8 * slab, last=[pltpu.HBM] * 6, room=42,
    )(coords, mode_table, quad_weight.reshape(ROWS, C), lin_weight, bias.reshape(1, C), features)
    got = send(far, ("core",), 1)

    def near(count, first, given, alias):
        return call(
            functools.partial(near_body, count, first), 4,
            [pltpu.VMEM((count * 2 * C + 16, C), BF), pltpu.VMEM((8 * C, pts), BF)],
            "near", [scr], 1, 2 * count * slab, last=[pltpu.VMEM if alias else pl.ANY], aliases={5: 1} if alias else {},
        )(index, quad, exy, ez, w, given)

    mine, basis = near(3, 1, linear, False)
    outs = call(pair_body, 2, [one(2 * C + 16, C, BF)] * 3, "pair")(mine, got)
    across = {s: send(outs[s - 1], ("x",), s) for s in FAR_LAST}
    mine, basis = near(1, 0, basis, True)
    keep, *outs = call(x_body, 5, [one(48, 2 * C, F32)] + [one(48, 2 * C, BF)] * 3, "x_sum")(
        mine, got, *[across[s] for s in FAR_LAST]
    )
    got = [send(outs[s - 1], ("z_hi",), s) for s in (2, 1, 3)]
    piece, total = call(filter_body, 5, [one(32, 2 * C, BF), one(8, C, F32)], "filter")(keep, *got, mode_weight)
    piece = gather_over(piece, ("z_hi",), 4)
    piece = gather_over(piece, ("x",), 4)
    other = send(piece, ("core",), 1)
    part = call(
        near_field_body, 2, pltpu.VMEM((C, pts), F32), "near_field", [pltpu.VMEM((C, 8 * C), BF)], flops=4 * slab
    )(piece, basis)
    f = call(turned_body, 1, one(C, 8 * C, BF), "turned")(other)
    def field(places, dtype, basis, part, last=False):
        chain = [] if last else [pltpu.VMEM(v.shape, v.dtype) for v in (basis, part)]
        return call(
            functools.partial(synthesis_body, places), 3, [one(len(places) * C, 512, dtype)] + chain, "synthesis",
            flops=len(places) * slab // 2, aliases={1: 1, 2: 2} if chain else {},
        )(f, basis, part)

    def merge(*pairs):
        return call(functools.partial(merge_body, pairs), 2, [one(C, 512, BF)] * len(pairs), "merge")

    out, far_basis, part = field(((1, 1), (1, 3)), BF, far_basis, part)
    beside = send(out, ("z_lo",), 1)
    out, far_basis, part = field(((0, 2), (1, 2)), BF, far_basis, part)
    across = send(out, ("y",), 2)
    (own,) = field(((0, 1), (0, 3), (1, 0), (0, 0)), F32, far_basis, part, True)
    one_step, three_steps = merge((0, 0), (1, 1))(own, beside)
    (out,) = merge((2, 1))(own, across)
    fields = [across, send(one_step, ("y",), 1), send(three_steps, ("y",), 3), send(out, ("z_lo",), 1)]
    return call(finish_body, 7, one(pts // 8, C, BF), "finish")(total, linear, own, *fields)


def solution(mesh):
    fine = Mesh(mesh.devices.reshape([SIZES[a] for a in ALL]), ALL)
    return jax.shard_map(
        on_device,
        mesh=fine,
        in_specs=(
            P(PTS, None),
            P(None, PTS),
            P(PTS),
            P(),
            P(ALL, None, None, None),
            P(),
            P(),
        ),
        out_specs=P(ALL, None),
        check_vma=False,
    )
```

```python
import functools
import math

import jax
import jax.numpy as jnp
from jax import lax
from jax.experimental import pallas as pl
from jax.experimental.pallas import tpu as pltpu
from jax.sharding import Mesh, PartitionSpec as P

SIZES = {"z_hi": 4, "x": 4, "core": 2, "y": 4, "z_lo": 2}
PTS = ("z_hi", "x", "core")
GRP = ("y", "z_lo")
ALL = PTS + GRP
FAR_LAST = (1, 3, 2)
C = 128
PITCH = C + 1
ROWS = 32
BF, F32 = jnp.bfloat16, jnp.float32
VM = pl.BlockSpec(memory_space=pltpu.VMEM)
SM = pl.BlockSpec(memory_space=pltpu.SMEM)


def call(body, n_in, out_shape, name, scratch=(), smem=0, flops=0, aliases={}, last=(), room=16):
    many = isinstance(out_shape, (list, tuple))
    return pl.pallas_call(
        body,
        in_specs=[SM] * smem + [VM] * n_in + [pl.BlockSpec(memory_space=m) for m in last],
        out_specs=[VM] * len(out_shape) if many else VM,
        out_shape=out_shape,
        scratch_shapes=list(scratch),
        compiler_params=pltpu.CompilerParams(vmem_limit_bytes=room * 2**20),
        input_output_aliases=aliases,
        cost_estimate=pl.CostEstimate(flops=flops, bytes_accessed=2**20, transcendentals=0),
        name=name,
    )


def send(value, axes, shift):
    n = 1
    for a in axes:
        n *= SIZES[a]
    return lax.ppermute(value, axes, [(j, (j + shift) % n) for j in range(n)])


def turn(x):
    h = math.pi * (x - jnp.round(x))
    q = h * h
    s = c = None
    for k in range(6, -1, -1):
        a = (-1) ** k / math.factorial(2 * k + 1)
        s = a if s is None else s * q + a
    for k in range(7, -1, -1):
        a = (-1) ** k / math.factorial(2 * k)
        c = a if c is None else c * q + a
    s = s * h
    return 1.0 - 2.0 * s * s, -2.0 * s * c


def times(a, b):
    return a[0] * b[0] - a[1] * b[1], a[0] * b[1] + a[1] * b[0]


def powers(x, n):
    one = turn(x)
    out = [(jnp.ones_like(x), jnp.zeros_like(x)), one]
    for k in range(2, n):
        out.append(times(out[k // 2], out[k - k // 2]))
    return out


def build_tables(coords, exy, ez, sl):
    for k, v in enumerate(powers(coords[2], 32)):
        ez[k, 0, sl], ez[k, 1, sl] = v
    px, py = powers(coords[0], 9), powers(coords[1], 9)
    signed = lambda p, k: p[k] if k >= 0 else (p[-k][0], -p[-k][1])
    for kx in range(-8, 8):
        for ky in range(-8, 8):
            k = (kx + 8) * 16 + ky + 8
            exy[k, 0, sl], exy[k, 1, sl] = times(signed(px, kx), signed(py, ky))


def lanes3(value):
    hi = value.astype(BF).astype(F32)
    mid = (value - hi).astype(BF).astype(F32)
    low = value - hi - mid
    lane = lax.broadcasted_iota(jnp.int32, (16, C), 1)
    return jnp.where(lane == 0, hi, jnp.where(lane == 1, mid, jnp.where(lane == 2, low, 0.0))).astype(BF)


def total_of(rows):
    lane = lax.broadcasted_iota(jnp.int32, (1, C), 1)
    return jnp.sum(jnp.where(lane < 3, rows[:1], 0.0), axis=1, keepdims=True)


def analyse(index, row, put_coef, put_basis, exy, ez, w, scr):
    @pl.loop(0, C // 16)
    def _(it):
        for u in range(16):
            m = it * 16 + u
            k = index[row, m]
            ixy, iz = lax.shift_right_logical(k, 5), lax.bitwise_and(k, 31)
            for j in range(ROWS // 8):
                sl = pl.ds(8 * j, 8)
                re, im = times((exy[ixy, 0, sl], exy[ixy, 1, sl]), (ez[iz, 0, sl], ez[iz, 1, sl]))
                scr[pl.ds(8 * j * PITCH + m, 8, stride=PITCH), :] = re
                scr[pl.ds((ROWS + 8 * j) * PITCH + m, 8, stride=PITCH), :] = im

    acc = None
    for k in range(4):
        cols = pl.ds(k * 1024, 1024)
        both = []
        for part in range(2):
            rows = [scr[pl.ds((part * ROWS + k * 8 + h) * PITCH, C), :].astype(BF) for h in range(8)]
            both.append(jnp.concatenate(rows, axis=1))
        both = jnp.concatenate(both, axis=0)
        put_basis(cols, both)
        term = jnp.dot(both, w[cols, :], preferred_element_type=F32)
        acc = term if acc is None else acc + term
    put_coef(acc.astype(BF))


def slabs(count, first, index, coef, basis, exy, ez, w, quad, scr):
    @pl.loop(0, count)
    def _(s):
        def put_coef(value):
            coef[pl.ds(pl.multiple_of(s * 2 * C, 2 * C), 2 * C), :] = value

        def put_basis(cols, value):
            basis[pl.ds(pl.multiple_of((first % 4 + s) * 2 * C, 2 * C), 2 * C), cols] = value

        analyse(index, first + s, put_coef, put_basis, exy, ez, w, scr)

    total = jnp.sum(jnp.sum(quad[...], axis=0, keepdims=True), axis=1, keepdims=True)
    coef[pl.ds(count * 2 * C, 16), :] = lanes3(total)


def pack_index(table, index):
    z, x, core = (lax.axis_index(a) for a in PTS)
    group = lax.axis_index("y") * 2 + lax.axis_index("z_lo")
    tile, within = group // 4, lax.rem(group, 4)
    part = lax.broadcasted_iota(jnp.int32, (1, C), 1) // 32
    for flip in range(2):
        for dx in range(4):
            row = jnp.zeros((1, C), jnp.int32)
            for dz in range(4):
                own = (lax.rem(z + dz, 4) * 4 + lax.rem(x + dx, 4)) * 2 + lax.rem(core + flip, 2)
                v = table[:, pl.ds(pl.multiple_of(own * 256 + tile * C, C), C)]
                k = ((v[0:1] + 8) * 16 + v[1:2] + 8) * 32 + v[2:3]
                k = pltpu.roll(k, lax.rem(dz - within + 4, 4) * 32, 1)
                row = jnp.where(part == dz, k, row)
            index[pl.ds(flip * 4 + dx, 1), :] = row


def first_body(*refs):
    given, (coef, basis, exy, ez, w, linear, quad, index) = refs[:6], refs[6:14]
    scr, coords, table, lin, bias, f, held, sems = refs[14:]
    here = (coords, table, quad, lin, bias, f)
    loads = [pltpu.make_async_copy(src, dst, sems.at[i]) for i, (src, dst) in enumerate(zip(given, here))]
    for load in loads:
        load.start()
    loads[0].wait()

    @pl.loop(0, ROWS // 8)
    def _(o):
        row = lambda i, r: coords[pl.ds(i, 1), pl.ds(pl.multiple_of((8 * o + r) * C, C), C)]
        at = [jnp.concatenate([row(i, r) for r in range(8)], axis=0) for i in range(3)]
        build_tables(at, exy, ez, pl.ds(pl.multiple_of(8 * o, 8), 8))

    loads[1].wait()
    pack_index(table, index)
    hold = pltpu.make_async_copy(index, held, sems.at[6])
    hold.start()
    for load in loads[2:]:
        load.wait()
    columns = quad[...].T
    for o in range(ROWS):
        rows = pl.ds(o * C, C)
        w[rows, :] = (f[rows, :].astype(F32) * columns[:, o : o + 1]).astype(BF)
    group = lax.axis_index("y") * 2 + lax.axis_index("z_lo")
    mine = f[pl.ds(pl.multiple_of(group * 512, 512), 512), :]
    linear[...] = jnp.dot(mine, lin[...], preferred_element_type=F32) + bias[...]
    hold.wait()
    slabs(4, 4, held, coef, basis, exy, ez, w, quad, scr)


def near_body(count, first, index, quad, exy, ez, w, given, coef, basis, scr):
    slabs(count, first, index, coef, basis, exy, ez, w, quad, scr)


def pair_body(own, got, *outs):
    tail = total_of(own[pl.ds(6 * C, 16), :].astype(F32) + got[pl.ds(8 * C, 16), :].astype(F32))
    for s, out in enumerate(outs):
        summed = own[pl.ds(s * 2 * C, 2 * C), :].astype(F32) + got[pl.ds((s + 1) * 2 * C, 2 * C), :].astype(F32)
        out[pl.ds(0, 2 * C), :] = summed.astype(BF)
        out[pl.ds(2 * C, 16), :] = lanes3(tail)


def x_body(own, got0, got1, got2, got3, keep, out1, out2, out3):
    body, rest = pl.ds(0, 2 * C), pl.ds(2 * C, 16)
    summed = own[body, :].astype(F32) + got0[body, :].astype(F32)
    tail = own[rest, :].astype(F32) + got0[pl.ds(8 * C, 16), :].astype(F32)
    for g in (got1, got2, got3):
        summed = summed + g[body, :].astype(F32)
        tail = tail + g[rest, :].astype(F32)
    tail = lanes3(total_of(tail))
    for part in range(2):
        cols = pl.ds(part * C, C)
        for s, ref in enumerate((keep, out1, out2, out3)):
            at = part * C + s * 32
            ref[pl.ds(0, 32), cols] = summed[at : at + 32].astype(ref.dtype)
            ref[pl.ds(32, 16), cols] = tail.astype(ref.dtype)


def filter_body(own, got1, got2, got3, weight, out, total):
    summed = own[...]
    for g in (got1, got2, got3):
        summed = summed + g[...].astype(F32)
    total[...] = jnp.broadcast_to(total_of(summed[32:, :C]), total.shape)
    row = lax.rem(lax.broadcasted_iota(jnp.int32, (16, 2 * C), 0), 8)
    for g in range(4):
        block = summed[8 * g : 8 * g + 8]
        lhs = jnp.concatenate([block[:, :C], block[:, C:]], axis=0).astype(BF)
        picked = jnp.zeros((16, 2 * C), F32)
        for i in range(8):
            m = 8 * g + i
            both = jnp.concatenate([weight[m, 0], weight[m, 1]], axis=1)
            picked = jnp.where(row == i, jnp.dot(lhs, both, preferred_element_type=F32), picked)
        real = picked[:8, :C] - picked[8:, C:]
        imag = picked[:8, C:] + picked[8:, :C]
        out[pl.ds(8 * g, 8), :] = jnp.concatenate([real, imag], axis=1).astype(BF)


def turned_body(src, out):
    for dx in range(4):
        for part in range(2):
            block = src[pl.ds(dx * C, C), pl.ds(part * C, C)].astype(F32).T
            out[:, pl.ds((dx * 2 + part) * C, C)] = block.astype(BF)


def near_field_body(src, basis, part, f):
    turned_body(src, f)
    for k in range(8):
        at = pl.ds(k * 512, 512)
        part[:, at] = jnp.dot(f[...], basis[:, at], preferred_element_type=F32)


def synthesis_body(places, f, basis, part, out, *_):
    y, z_lo = lax.axis_index("y"), lax.axis_index("z_lo")
    for i, (flip, dy) in enumerate(places):
        owner = lax.rem(y + dy, 4) * 2 + lax.rem(z_lo + flip, 2)
        at = pl.ds(pl.multiple_of(owner * 512, 512), 512)
        value = part[:, at] + jnp.dot(f[...], basis[:, at], preferred_element_type=F32)
        out[pl.ds(i * C, C), :] = value.astype(out.dtype)


def merge_body(pairs, own, got, *outs):
    for (mine, theirs), out in zip(pairs, outs, strict=True):
        out[...] = (own[pl.ds(mine * C, C), :] + got[pl.ds(theirs * C, C), :].astype(F32)).astype(BF)


def finish_body(total, linear, own, *rest):
    *blocks, out = rest
    summed = own[pl.ds(3 * C, C), :]
    for b in blocks:
        summed = summed + b[pl.ds(0, C), :].astype(F32)
    scaled = summed / total[0:1, 0:1]
    for k in range(4):
        rows = pl.ds(k * C, C)
        pre = scaled[:, k * C : k * C + C].T + linear[rows, :]
        out[rows, :] = (0.5 * pre * (1.0 + lax.erf(pre * math.sqrt(0.5)))).astype(BF)


def join_body(piece, *rest):
    *got, out = rest
    rows = piece.shape[0]
    for s, ref in zip((0, *FAR_LAST), (piece, *got)):
        out[pl.ds(s * rows, rows), :] = ref[...]


def gather_over(piece, axes, n):
    got = [send(piece, axes, n - s) for s in FAR_LAST]
    shape = jax.ShapeDtypeStruct((n * piece.shape[0], piece.shape[1]), piece.dtype)
    return call(join_body, n, shape, "join")(piece, *got)


def on_device(features, coords, quad_weight, mode_table, mode_weight, lin_weight, bias):
    pts = features.shape[0]
    scr = pltpu.VMEM((2 * ROWS * PITCH, C), F32)
    one = lambda rows, cols, dt: jax.ShapeDtypeStruct((rows, cols), dt)
    slab = 2 * 2 * C * pts * C
    far, far_basis, exy, ez, w, linear, quad, index = call(
        first_body, 0,
        [pltpu.VMEM((8 * C + 16, C), BF), pltpu.VMEM((8 * C, pts), BF), pltpu.VMEM((256, 2, ROWS, C), F32),
         pltpu.VMEM((32, 2, ROWS, C), F32), pltpu.VMEM((pts, C), BF), pltpu.VMEM((pts // 8, C), F32),
         pltpu.VMEM((ROWS, C), F32), pltpu.VMEM((8, C), jnp.int32)],
        "first",
        [scr, pltpu.VMEM((3, pts), F32), pltpu.VMEM((3, 8192), jnp.int32), pltpu.VMEM((C, C), BF), pltpu.VMEM((1, C), F32),
         pltpu.VMEM((pts, C), BF), pltpu.SMEM((8, C), jnp.int32), pltpu.SemaphoreType.DMA((7,))],
        0, 8 * slab, last=[pltpu.HBM] * 6, room=42,
    )(coords, mode_table, quad_weight.reshape(ROWS, C), lin_weight, bias.reshape(1, C), features)
    got = send(far, ("core",), 1)

    def near(count, first, given, alias):
        return call(
            functools.partial(near_body, count, first), 4,
            [pltpu.VMEM((count * 2 * C + 16, C), BF), pltpu.VMEM((8 * C, pts), BF)],
            "near", [scr], 1, 2 * count * slab, last=[pltpu.VMEM if alias else pl.ANY], aliases={5: 1} if alias else {},
        )(index, quad, exy, ez, w, given)

    mine, basis = near(3, 1, linear, False)
    outs = call(pair_body, 2, [one(2 * C + 16, C, BF)] * 3, "pair")(mine, got)
    across = {s: send(outs[s - 1], ("x",), s) for s in (2, 1, 3)}
    mine, basis = near(1, 0, basis, True)
    keep, *outs = call(x_body, 5, [one(48, 2 * C, F32)] + [one(48, 2 * C, BF)] * 3, "x_sum")(
        mine, got, *[across[s] for s in (2, 1, 3)]
    )
    got = [send(outs[s - 1], ("z_hi",), s) for s in (2, 1, 3)]
    piece, total = call(filter_body, 5, [one(32, 2 * C, BF), one(8, C, F32)], "filter")(keep, *got, mode_weight)
    piece = gather_over(piece, ("z_hi",), 4)
    piece = gather_over(piece, ("x",), 4)
    other = send(piece, ("core",), 1)
    part = call(
        near_field_body, 2, pltpu.VMEM((C, pts), F32), "near_field", [pltpu.VMEM((C, 8 * C), BF)], flops=4 * slab
    )(piece, basis)
    f = call(turned_body, 1, one(C, 8 * C, BF), "turned")(other)
    def field(places, dtype, basis, part, last=False):
        chain = [] if last else [pltpu.VMEM(v.shape, v.dtype) for v in (basis, part)]
        return call(
            functools.partial(synthesis_body, places), 3, [one(len(places) * C, 512, dtype)] + chain, "synthesis",
            flops=len(places) * slab // 2, aliases={1: 1, 2: 2} if chain else {},
        )(f, basis, part)

    def merge(*pairs):
        return call(functools.partial(merge_body, pairs), 2, [one(C, 512, BF)] * len(pairs), "merge")

    out, far_basis, part = field(((0, 2), (1, 2)), BF, far_basis, part)
    across = send(out, ("y",), 2)
    out, far_basis, part = field(((1, 1), (1, 3)), BF, far_basis, part)
    beside = send(out, ("z_lo",), 1)
    (own,) = field(((0, 1), (0, 3), (1, 0), (0, 0)), F32, far_basis, part, True)
    one_step, three_steps = merge((0, 0), (1, 1))(own, beside)
    (out,) = merge((2, 1))(own, across)
    fields = [across, send(one_step, ("y",), 1), send(three_steps, ("y",), 3), send(out, ("z_lo",), 1)]
    return call(finish_body, 7, one(pts // 8, C, BF), "finish")(total, linear, own, *fields)


def solution(mesh):
    fine = Mesh(mesh.devices.reshape([SIZES[a] for a in ALL]), ALL)
    return jax.shard_map(
        on_device,
        mesh=fine,
        in_specs=(
            P(PTS, None),
            P(None, PTS),
            P(PTS),
            P(),
            P(ALL, None, None, None),
            P(),
            P(),
        ),
        out_specs=P(ALL, None),
        check_vma=False,
    )
```

```python
import functools
import math

import jax
import jax.numpy as jnp
from jax import lax
from jax.experimental import pallas as pl
from jax.experimental.pallas import tpu as pltpu
from jax.sharding import Mesh, PartitionSpec as P

SIZES = {"z_hi": 4, "x": 4, "core": 2, "y": 4, "z_lo": 2}
PTS = ("z_hi", "x", "core")
GRP = ("y", "z_lo")
ALL = PTS + GRP
FAR_LAST = (1, 3, 2)
C = 128
PITCH = C + 1
ROWS = 32
BF, F32 = jnp.bfloat16, jnp.float32
VM = pl.BlockSpec(memory_space=pltpu.VMEM)
SM = pl.BlockSpec(memory_space=pltpu.SMEM)


def call(body, n_in, out_shape, name, scratch=(), smem=0, flops=0, aliases={}, last=(), room=16):
    many = isinstance(out_shape, (list, tuple))
    return pl.pallas_call(
        body,
        in_specs=[SM] * smem + [VM] * n_in + [pl.BlockSpec(memory_space=m) for m in last],
        out_specs=[VM] * len(out_shape) if many else VM,
        out_shape=out_shape,
        scratch_shapes=list(scratch),
        compiler_params=pltpu.CompilerParams(vmem_limit_bytes=room * 2**20),
        input_output_aliases=aliases,
        cost_estimate=pl.CostEstimate(flops=flops, bytes_accessed=2**20, transcendentals=0),
        name=name,
    )


def send(value, axes, shift):
    n = 1
    for a in axes:
        n *= SIZES[a]
    return lax.ppermute(value, axes, [(j, (j + shift) % n) for j in range(n)])


def turn(x):
    h = math.pi * (x - jnp.round(x))
    q = h * h
    s = c = None
    for k in range(6, -1, -1):
        a = (-1) ** k / math.factorial(2 * k + 1)
        s = a if s is None else s * q + a
    for k in range(7, -1, -1):
        a = (-1) ** k / math.factorial(2 * k)
        c = a if c is None else c * q + a
    s = s * h
    return 1.0 - 2.0 * s * s, -2.0 * s * c


def times(a, b):
    return a[0] * b[0] - a[1] * b[1], a[0] * b[1] + a[1] * b[0]


def powers(x, n):
    one = turn(x)
    out = [(jnp.ones_like(x), jnp.zeros_like(x)), one]
    for k in range(2, n):
        out.append(times(out[k // 2], out[k - k // 2]))
    return out


def build_tables(coords, exy, ez, sl):
    for k, v in enumerate(powers(coords[2], 32)):
        ez[k, 0, sl], ez[k, 1, sl] = v
    px, py = powers(coords[0], 9), powers(coords[1], 9)
    signed = lambda p, k: p[k] if k >= 0 else (p[-k][0], -p[-k][1])
    for kx in range(-8, 8):
        for ky in range(-8, 8):
            k = (kx + 8) * 16 + ky + 8
            exy[k, 0, sl], exy[k, 1, sl] = times(signed(px, kx), signed(py, ky))


def lanes3(value):
    hi = value.astype(BF).astype(F32)
    mid = (value - hi).astype(BF).astype(F32)
    low = value - hi - mid
    lane = lax.broadcasted_iota(jnp.int32, (16, C), 1)
    return jnp.where(lane == 0, hi, jnp.where(lane == 1, mid, jnp.where(lane == 2, low, 0.0))).astype(BF)


def total_of(rows):
    lane = lax.broadcasted_iota(jnp.int32, (1, C), 1)
    return jnp.sum(jnp.where(lane < 3, rows[:1], 0.0), axis=1, keepdims=True)


def analyse(index, row, put_coef, put_basis, exy, ez, w, scr):
    @pl.loop(0, C // 32)
    def _(it):
        for u in range(32):
            m = it * 32 + u
            k = index[row, m]
            ixy, iz = lax.shift_right_logical(k, 5), lax.bitwise_and(k, 31)
            for j in range(ROWS // 8):
                sl = pl.ds(8 * j, 8)
                re, im = times((exy[ixy, 0, sl], exy[ixy, 1, sl]), (ez[iz, 0, sl], ez[iz, 1, sl]))
                scr[pl.ds(8 * j * PITCH + m, 8, stride=PITCH), :] = re
                scr[pl.ds((ROWS + 8 * j) * PITCH + m, 8, stride=PITCH), :] = im

    acc = None
    for k in range(4):
        cols = pl.ds(k * 1024, 1024)
        both = []
        for part in range(2):
            rows = [scr[pl.ds((part * ROWS + k * 8 + h) * PITCH, C), :].astype(BF) for h in range(8)]
            both.append(jnp.concatenate(rows, axis=1))
        both = jnp.concatenate(both, axis=0)
        put_basis(cols, both)
        term = jnp.dot(both, w[cols, :], preferred_element_type=F32)
        acc = term if acc is None else acc + term
    put_coef(acc.astype(BF))


def slabs(count, first, index, coef, basis, exy, ez, w, quad, scr):
    @pl.loop(0, count)
    def _(s):
        def put_coef(value):
            coef[pl.ds(pl.multiple_of(s * 2 * C, 2 * C), 2 * C), :] = value

        def put_basis(cols, value):
            basis[pl.ds(pl.multiple_of((first % 4 + s) * 2 * C, 2 * C), 2 * C), cols] = value

        analyse(index, first + s, put_coef, put_basis, exy, ez, w, scr)

    total = jnp.sum(jnp.sum(quad[...], axis=0, keepdims=True), axis=1, keepdims=True)
    coef[pl.ds(count * 2 * C, 16), :] = lanes3(total)


def pack_index(table, index):
    z, x, core = (lax.axis_index(a) for a in PTS)
    group = lax.axis_index("y") * 2 + lax.axis_index("z_lo")
    tile, within = group // 4, lax.rem(group, 4)
    part = lax.broadcasted_iota(jnp.int32, (1, C), 1) // 32
    for flip in range(2):
        for dx in range(4):
            row = jnp.zeros((1, C), jnp.int32)
            for dz in range(4):
                own = (lax.rem(z + dz, 4) * 4 + lax.rem(x + dx, 4)) * 2 + lax.rem(core + flip, 2)
                v = table[:, pl.ds(pl.multiple_of(own * 256 + tile * C, C), C)]
                k = ((v[0:1] + 8) * 16 + v[1:2] + 8) * 32 + v[2:3]
                k = pltpu.roll(k, lax.rem(dz - within + 4, 4) * 32, 1)
                row = jnp.where(part == dz, k, row)
            index[pl.ds(flip * 4 + dx, 1), :] = row


def first_body(*refs):
    given, (coef, basis, exy, ez, w, linear, quad, index) = refs[:6], refs[6:14]
    scr, coords, table, lin, bias, f, held, sems = refs[14:]
    here = (coords, table, quad, lin, bias, f)
    loads = [pltpu.make_async_copy(src, dst, sems.at[i]) for i, (src, dst) in enumerate(zip(given, here))]
    for load in loads:
        load.start()
    loads[0].wait()

    @pl.loop(0, ROWS // 8)
    def _(o):
        row = lambda i, r: coords[pl.ds(i, 1), pl.ds(pl.multiple_of((8 * o + r) * C, C), C)]
        at = [jnp.concatenate([row(i, r) for r in range(8)], axis=0) for i in range(3)]
        build_tables(at, exy, ez, pl.ds(pl.multiple_of(8 * o, 8), 8))

    loads[1].wait()
    pack_index(table, index)
    hold = pltpu.make_async_copy(index, held, sems.at[6])
    hold.start()
    for load in loads[2:]:
        load.wait()
    columns = quad[...].T
    for o in range(ROWS):
        rows = pl.ds(o * C, C)
        w[rows, :] = (f[rows, :].astype(F32) * columns[:, o : o + 1]).astype(BF)
    group = lax.axis_index("y") * 2 + lax.axis_index("z_lo")
    mine = f[pl.ds(pl.multiple_of(group * 512, 512), 512), :]
    linear[...] = jnp.dot(mine, lin[...], preferred_element_type=F32) + bias[...]
    hold.wait()
    slabs(4, 4, held, coef, basis, exy, ez, w, quad, scr)


def near_body(count, first, index, quad, exy, ez, w, given, coef, basis, scr):
    slabs(count, first, index, coef, basis, exy, ez, w, quad, scr)


def pair_body(own, got, *outs):
    tail = total_of(own[pl.ds(6 * C, 16), :].astype(F32) + got[pl.ds(8 * C, 16), :].astype(F32))
    for s, out in enumerate(outs):
        summed = own[pl.ds(s * 2 * C, 2 * C), :].astype(F32) + got[pl.ds((s + 1) * 2 * C, 2 * C), :].astype(F32)
        out[pl.ds(0, 2 * C), :] = summed.astype(BF)
        out[pl.ds(2 * C, 16), :] = lanes3(tail)


def x_body(own, got0, got1, got2, got3, keep, out1, out2, out3):
    body, rest = pl.ds(0, 2 * C), pl.ds(2 * C, 16)
    summed = own[body, :].astype(F32) + got0[body, :].astype(F32)
    tail = own[rest, :].astype(F32) + got0[pl.ds(8 * C, 16), :].astype(F32)
    for g in (got1, got2, got3):
        summed = summed + g[body, :].astype(F32)
        tail = tail + g[rest, :].astype(F32)
    tail = lanes3(total_of(tail))
    for part in range(2):
        cols = pl.ds(part * C, C)
        for s, ref in enumerate((keep, out1, out2, out3)):
            at = part * C + s * 32
            ref[pl.ds(0, 32), cols] = summed[at : at + 32].astype(ref.dtype)
            ref[pl.ds(32, 16), cols] = tail.astype(ref.dtype)


def filter_body(own, got1, got2, got3, weight, out, total):
    summed = own[...]
    for g in (got1, got2, got3):
        summed = summed + g[...].astype(F32)
    total[...] = jnp.broadcast_to(total_of(summed[32:, :C]), total.shape)
    row = lax.rem(lax.broadcasted_iota(jnp.int32, (16, 2 * C), 0), 8)
    for g in range(4):
        block = summed[8 * g : 8 * g + 8]
        lhs = jnp.concatenate([block[:, :C], block[:, C:]], axis=0).astype(BF)
        picked = jnp.zeros((16, 2 * C), F32)
        for i in range(8):
            m = 8 * g + i
            both = jnp.concatenate([weight[m, 0], weight[m, 1]], axis=1)
            picked = jnp.where(row == i, jnp.dot(lhs, both, preferred_element_type=F32), picked)
        real = picked[:8, :C] - picked[8:, C:]
        imag = picked[:8, C:] + picked[8:, :C]
        out[pl.ds(8 * g, 8), :] = jnp.concatenate([real, imag], axis=1).astype(BF)


def turned_body(src, out):
    for dx in range(4):
        for part in range(2):
            block = src[pl.ds(dx * C, C), pl.ds(part * C, C)].astype(F32).T
            out[:, pl.ds((dx * 2 + part) * C, C)] = block.astype(BF)


def near_field_body(src, basis, part, f):
    turned_body(src, f)
    for k in range(8):
        at = pl.ds(k * 512, 512)
        part[:, at] = jnp.dot(f[...], basis[:, at], preferred_element_type=F32)


def synthesis_body(places, f, basis, part, out, *_):
    y, z_lo = lax.axis_index("y"), lax.axis_index("z_lo")
    for i, (flip, dy) in enumerate(places):
        owner = lax.rem(y + dy, 4) * 2 + lax.rem(z_lo + flip, 2)
        at = pl.ds(pl.multiple_of(owner * 512, 512), 512)
        value = part[:, at] + jnp.dot(f[...], basis[:, at], preferred_element_type=F32)
        out[pl.ds(i * C, C), :] = value.astype(out.dtype)


def merge_body(pairs, own, got, *outs):
    for (mine, theirs), out in zip(pairs, outs, strict=True):
        out[...] = (own[pl.ds(mine * C, C), :] + got[pl.ds(theirs * C, C), :].astype(F32)).astype(BF)


def finish_body(total, linear, own, *rest):
    *blocks, out = rest
    summed = own[pl.ds(3 * C, C), :]
    for b in blocks:
        summed = summed + b[pl.ds(0, C), :].astype(F32)
    scaled = summed / total[0:1, 0:1]
    for k in range(4):
        rows = pl.ds(k * C, C)
        pre = scaled[:, k * C : k * C + C].T + linear[rows, :]
        out[rows, :] = (0.5 * pre * (1.0 + lax.erf(pre * math.sqrt(0.5)))).astype(BF)


def join_body(piece, *rest):
    *got, out = rest
    rows = piece.shape[0]
    for s, ref in zip((0, *FAR_LAST), (piece, *got)):
        out[pl.ds(s * rows, rows), :] = ref[...]


def gather_over(piece, axes, n):
    got = [send(piece, axes, n - s) for s in FAR_LAST]
    shape = jax.ShapeDtypeStruct((n * piece.shape[0], piece.shape[1]), piece.dtype)
    return call(join_body, n, shape, "join")(piece, *got)


def on_device(features, coords, quad_weight, mode_table, mode_weight, lin_weight, bias):
    pts = features.shape[0]
    scr = pltpu.VMEM((2 * ROWS * PITCH, C), F32)
    one = lambda rows, cols, dt: jax.ShapeDtypeStruct((rows, cols), dt)
    slab = 2 * 2 * C * pts * C
    far, far_basis, exy, ez, w, linear, quad, index = call(
        first_body, 0,
        [pltpu.VMEM((8 * C + 16, C), BF), pltpu.VMEM((8 * C, pts), BF), pltpu.VMEM((256, 2, ROWS, C), F32),
         pltpu.VMEM((32, 2, ROWS, C), F32), pltpu.VMEM((pts, C), BF), pltpu.VMEM((pts // 8, C), F32),
         pltpu.VMEM((ROWS, C), F32), pltpu.VMEM((8, C), jnp.int32)],
        "first",
        [scr, pltpu.VMEM((3, pts), F32), pltpu.VMEM((3, 8192), jnp.int32), pltpu.VMEM((C, C), BF), pltpu.VMEM((1, C), F32),
         pltpu.VMEM((pts, C), BF), pltpu.SMEM((8, C), jnp.int32), pltpu.SemaphoreType.DMA((7,))],
        0, 8 * slab, last=[pltpu.HBM] * 6, room=42,
    )(coords, mode_table, quad_weight.reshape(ROWS, C), lin_weight, bias.reshape(1, C), features)
    got = send(far, ("core",), 1)

    def near(count, first, given, alias):
        return call(
            functools.partial(near_body, count, first), 4,
            [pltpu.VMEM((count * 2 * C + 16, C), BF), pltpu.VMEM((8 * C, pts), BF)],
            "near", [scr], 1, 2 * count * slab, last=[pltpu.VMEM if alias else pl.ANY], aliases={5: 1} if alias else {},
        )(index, quad, exy, ez, w, given)

    mine, basis = near(3, 1, linear, False)
    outs = call(pair_body, 2, [one(2 * C + 16, C, BF)] * 3, "pair")(mine, got)
    across = {s: send(outs[s - 1], ("x",), s) for s in (2, 1, 3)}
    mine, basis = near(1, 0, basis, True)
    keep, *outs = call(x_body, 5, [one(48, 2 * C, F32)] + [one(48, 2 * C, BF)] * 3, "x_sum")(
        mine, got, *[across[s] for s in (2, 1, 3)]
    )
    got = [send(outs[s - 1], ("z_hi",), s) for s in (2, 1, 3)]
    piece, total = call(filter_body, 5, [one(32, 2 * C, BF), one(8, C, F32)], "filter")(keep, *got, mode_weight)
    piece = gather_over(piece, ("z_hi",), 4)
    piece = gather_over(piece, ("x",), 4)
    other = send(piece, ("core",), 1)
    part = call(
        near_field_body, 2, pltpu.VMEM((C, pts), F32), "near_field", [pltpu.VMEM((C, 8 * C), BF)], flops=4 * slab
    )(piece, basis)
    f = call(turned_body, 1, one(C, 8 * C, BF), "turned")(other)
    def field(places, dtype, basis, part, last=False):
        chain = [] if last else [pltpu.VMEM(v.shape, v.dtype) for v in (basis, part)]
        return call(
            functools.partial(synthesis_body, places), 3, [one(len(places) * C, 512, dtype)] + chain, "synthesis",
            flops=len(places) * slab // 2, aliases={1: 1, 2: 2} if chain else {},
        )(f, basis, part)

    def merge(*pairs):
        return call(functools.partial(merge_body, pairs), 2, [one(C, 512, BF)] * len(pairs), "merge")

    out, far_basis, part = field(((0, 2), (1, 2)), BF, far_basis, part)
    across = send(out, ("y",), 2)
    out, far_basis, part = field(((1, 1), (1, 3)), BF, far_basis, part)
    beside = send(out, ("z_lo",), 1)
    (own,) = field(((0, 1), (0, 3), (1, 0), (0, 0)), F32, far_basis, part, True)
    one_step, three_steps = merge((0, 0), (1, 1))(own, beside)
    (out,) = merge((2, 1))(own, across)
    fields = [across, send(one_step, ("y",), 1), send(three_steps, ("y",), 3), send(out, ("z_lo",), 1)]
    return call(finish_body, 7, one(pts // 8, C, BF), "finish")(total, linear, own, *fields)


def solution(mesh):
    fine = Mesh(mesh.devices.reshape([SIZES[a] for a in ALL]), ALL)
    return jax.shard_map(
        on_device,
        mesh=fine,
        in_specs=(
            P(PTS, None),
            P(None, PTS),
            P(PTS),
            P(),
            P(ALL, None, None, None),
            P(),
            P(),
        ),
        out_specs=P(ALL, None),
        check_vma=False,
    )
```
